32 devices in a mesh: replica: 4 (over y, core), fsdp: 8 (over z, x).
Axes of the slice: x: 2, y: 2, z: 4, core: 2. Of those that a mesh axis runs over, the one named last changes fastest.
Arguments:
- gradients: bfloat16 [4, 1024, 8192], P('replica', 'fsdp'), may hold values from -6 to 6
- left_factor: float32 [8, 2, 2, 512, 512], P('fsdp', None, None, 'replica'), may hold values from -6 to 6
- right_factor: float32 [8, 2, 2, 512, 512], P('fsdp', None, None, 'replica'), may hold values from -6 to 6
- left_root: bfloat16 [8, 2, 2, 512, 512], P('fsdp', None, None, 'replica'), may hold values from -0.25 to 0.25
- right_root: bfloat16 [8, 2, 2, 512, 512], P('fsdp'), may hold values from -0.25 to 0.25
- owner_table: int32 [2, 16], replicated, may hold values from 0 to 7, as said below
Outputs:
- left_next: float32 [8, 2, 2, 512, 512], P('fsdp', None, None, 'replica')
- right_next: float32 [8, 2, 2, 512, 512], P('fsdp', None, None, 'replica')
- update: bfloat16 [8, 2, 2, 512, 512], P('fsdp', None, None, 'replica')
The draws below stay inside these ranges and needn't reach their ends.
Inputs may be any that keep to these rules, and one draw needn't show every extreme that they name: In each row of owner_table no owner is named more than 2 times.
All inputs are finite; a program needn't handle non-finite values.
Results may differ from the reference program's by a relative error of at most 0.02.
Values may be sent and summed in bfloat16 or wider, within the bound.
A program may use at most 64 MiB of HBM per device.

```python
import jax
import jax.numpy as jnp
from jax import lax

COLS = 8192
BS = 512
ROWS = 1024
MOST = 2
N_REPLICA = 4
N_FSDP = 8


def draw_gradients(key, part):
    key = jax.random.fold_in(key, 11)
    noise_key, row_key, col_key = jax.random.split(key, 3)
    row_part = jax.random.truncated_normal(row_key, -3.0, 3.0, (ROWS,), jnp.float32)
    col_part = jax.random.truncated_normal(col_key, -3.0, 3.0, (COLS,), jnp.float32)
    noise = 0.35 * jax.random.truncated_normal(noise_key, -6.0, 6.0, (N_REPLICA, ROWS, COLS), jnp.float32)
    strength = 1.2
    shared = strength / N_REPLICA * row_part[:, None] * col_part[None, :]
    return (noise + shared[None, :, :]).astype(jnp.bfloat16)


def draw_owner_table(key, part):
    key = jax.random.fold_in(key, 7)
    first, second, third = jax.random.split(key, 3)
    block_rows = ROWS // BS
    block_cols = COLS // BS
    owners = N_FSDP
    depth = MOST
    contender_list = owners * depth
    preferred_pick = jax.random.permutation(first, owners) < max(1, owners // 8)
    block_owner_lookup = jnp.arange(contender_list, dtype=jnp.int32) // depth
    extra_credit = jnp.where(preferred_pick[block_owner_lookup], 2 ** 17, 0).astype(jnp.int32)
    random_jitter = jax.random.randint(second, (block_rows, contender_list), 0, 2 ** 16, dtype=jnp.int32)
    ranking_values = (random_jitter + extra_credit[None, :]) * contender_list + jnp.arange(contender_list, dtype=jnp.int32)[None, :]
    unused, chosen = lax.top_k(ranking_values, block_cols)
    picked = block_owner_lookup[chosen]
    shuffle = jax.random.randint(third, (block_rows, block_cols), 0, 2 ** 16, dtype=jnp.int32) * block_cols + jnp.arange(block_cols, dtype=jnp.int32)[None, :]
    ordering = jnp.argsort(shuffle, axis=1)
    return jnp.take_along_axis(picked, ordering, axis=1).astype(jnp.int32)


def block_levels(stream_key, shape, pieces, smallest, high):
    def one(dim, parts):
        heights = jax.random.uniform(jax.random.fold_in(jax.random.fold_in(stream_key, 6), dim), (parts,), jnp.float32, smallest / len(pieces), high / len(pieces))
        return jnp.repeat(jnp.exp(heights), shape[dim] // parts).reshape((-1,) + (1,) * (len(shape) - dim - 1))

    level = one(*pieces[0])
    for cut in pieces[1:]:
        level = level * one(*cut)
    return level


def bell_draw(own_key, extent, deviation, bound, shards=(), kind=jnp.bfloat16):
    array = jax.random.normal(own_key, extent, jnp.float32) * deviation
    if len(shards) > 0:
        array = block_levels(own_key, extent, shards, -0.22, 0.18) * array
    return jnp.clip(array, min=-bound, max=bound).astype(kind)


def setup_inputs(seed: int = 0) -> dict:
    keys = jax.random.split(jax.random.key(seed), 7)
    gradients = draw_gradients(jax.random.fold_in(keys[6], 71), 0)
    left_factor = bell_draw(keys[1], (N_FSDP, MOST, ROWS // BS, BS, BS), 0.5, 6.0, ((0, 8), (3, 4)), jnp.float32)
    right_factor = bell_draw(keys[2], (N_FSDP, MOST, ROWS // BS, BS, BS), 0.5, 6.0, ((0, 8), (3, 4)), jnp.float32)
    left_root = bell_draw(keys[3], (N_FSDP, MOST, ROWS // BS, BS, BS), BS ** -0.5, 0.25, ((0, 8), (3, 4)))
    right_root = bell_draw(keys[4], (N_FSDP, MOST, ROWS // BS, BS, BS), BS ** -0.5, 0.25, ((0, 8),))
    owner_table = draw_owner_table(jax.random.fold_in(keys[6], 71), 0)
    return dict(gradients=gradients, left_factor=left_factor, right_factor=right_factor, left_root=left_root, right_root=right_root, owner_table=owner_table)


decay_rate = 0.9


def slot_table(owner_table, owner_count, slot_depth):
    block_cols = owner_table.shape[1]
    owner_match = (owner_table[:, :, None] == jnp.arange(owner_count, dtype=jnp.int32)[None, None, :]).astype(jnp.int32)
    earlier = (jnp.cumsum(owner_match, axis=1) - owner_match).astype(jnp.int32)
    column_rank = jnp.sum(earlier * owner_match, axis=2).astype(jnp.int32)
    slot_match = (column_rank[:, :, None] == jnp.arange(slot_depth, dtype=jnp.int32)[None, None, :]).astype(jnp.int32)
    joint = owner_match[:, :, None, :] * slot_match[:, :, :, None]
    column_ids = jnp.arange(block_cols, dtype=jnp.int32)[None, :, None, None]
    col_table = jnp.sum(joint * column_ids, axis=1).astype(jnp.int32)
    col_valid = jnp.sum(joint, axis=1).astype(jnp.int32)
    return col_table, col_valid


def reference(gradients, left_factor, right_factor, left_root, right_root, owner_table):
    summed = jnp.sum(gradients.astype(jnp.float32), axis=0).astype(jnp.bfloat16)
    block_rows = ROWS // BS
    block_cols = COLS // BS
    tiles = summed.reshape(block_rows, BS, block_cols, BS).transpose(0, 2, 1, 3)
    col_table, col_valid = slot_table(owner_table, N_FSDP, MOST)
    row_ids = jnp.arange(block_rows, dtype=jnp.int32)[:, None]
    scale = (1.0 - decay_rate) / BS

    def per_owner(items):
        owner, left_one, single_right_factor, lroot_one, rroot_one = items
        picks = jnp.take(col_table, owner, axis=2)
        live = jnp.take(col_valid, owner, axis=2)
        chosen = tiles[row_ids, picks]
        chosen = chosen * live[:, :, None, None].astype(jnp.bfloat16)
        chosen = jnp.transpose(chosen, (1, 0, 2, 3)).astype(jnp.float32)
        stat_left = jnp.einsum('kjab,kjcb->kjac', chosen, chosen)
        stat_right = jnp.einsum('kjba,kjbc->kjac', chosen, chosen)
        left_new = decay_rate * left_one + scale * stat_left
        right_new = decay_rate * single_right_factor + scale * stat_right
        half = jnp.einsum('kjab,kjbc->kjac', lroot_one.astype(jnp.float32), chosen).astype(jnp.bfloat16)
        result = jnp.einsum('kjab,kjbc->kjac', half.astype(jnp.float32), rroot_one.astype(jnp.float32)).astype(jnp.bfloat16)
        return left_new, right_new, result

    owners = jnp.arange(N_FSDP, dtype=jnp.int32)
    left_next, right_next, update = lax.map(per_owner, (owners, left_factor, right_factor, left_root, right_root))
    return (left_next, right_next, update)
```

```python
import functools

import jax
import jax.numpy as jnp
from jax import lax
from jax.experimental import pallas as pl
from jax.experimental.pallas import tpu as pltpu
from jax.sharding import PartitionSpec as P

decay_rate = 0.9
MESH = pl.DeviceIdType.MESH
CORES = 2
HALVES = 2


def exchange(geo, table, grad, out, strip, cols, live, pair_out, pair_in, near_out, near_in, ready, blocks,
             load_sem, s1, r1, s2, r2, s3, r3, s4, r4, s5, r5, out_sem):
    depth, owners, ways, piece, width, halves, per_block, columns = geo
    part = width // halves
    chunks = depth * halves
    f = lax.axis_index("fsdp")
    r = lax.axis_index("replica")
    c, y = lax.rem(r, CORES), lax.div(r, CORES)
    mate = y * CORES + (1 - c)

    loads = []
    for col in range(columns):
        load = pltpu.make_async_copy(grad.at[0, :, pl.ds(col * width, width)], strip.at[col], load_sem.at[col])
        load.start()
        loads.append(load)

    def far_y(step):
        return lax.rem(y + step, ways)

    def far_f(step):
        return lax.rem(f + step, owners)

    barrier = pltpu.get_barrier_semaphore()
    pl.semaphore_signal(barrier, inc=1, device_id={"replica": mate}, device_id_type=MESH)
    for step in range(1, ways):
        pl.semaphore_signal(barrier, inc=1, device_id={"replica": far_y(step) * CORES + c}, device_id_type=MESH)
    for step in range(1, owners):
        pl.semaphore_signal(barrier, inc=1, device_id={"fsdp": far_f(step)}, device_id_type=MESH)

    row = lax.div(f, per_block)

    def place(d, carry):
        seen = jnp.int32(0)
        spot = [jnp.int32(0)] * depth
        for col in range(columns):
            hit = table[row, col] == d
            for k in range(depth):
                spot[k] = jnp.where(hit & (seen == k), col, spot[k])
            seen = seen + hit.astype(jnp.int32)
        for k in range(depth):
            cols[k, d] = spot[k]
            live[k, d] = jnp.where(seen > k, 1, 0)
        return carry

    lax.fori_loop(0, owners, place, 0)
    pl.semaphore_wait(barrier, 1 + (ways - 1) + (owners - 1))
    for load in loads:
        load.wait()

    def mine(n, d, q, core):
        k, h = n // halves, n % halves
        top = pl.multiple_of((q * CORES + core) * piece, 16)
        return strip[cols[k, d], pl.ds(top, piece), h * part:(h + 1) * part]

    pending = []

    def send(src, dst, s, t, **to):
        copy = pltpu.make_async_remote_copy(
            src_ref=src, dst_ref=dst, send_sem=s, recv_sem=t, device_id=to, device_id_type=MESH
        )
        copy.start()
        pending.append(copy)
        return copy

    first = []
    for n in range(chunks):
        def fill(d, carry):
            for q in range(ways):
                pair_out[n, q, d] = mine(n, d, q, 1 - c)
            return carry

        lax.fori_loop(0, owners, fill, 0)
        first.append(send(pair_out.at[n], pair_in.at[n], s1.at[n], r1.at[n], replica=mate))

    second = []
    for n in range(chunks):
        first[n].wait_recv()
        sent = []
        for step in range(1, ways):
            q = far_y(step)

            def add(d, carry):
                total = mine(n, d, q, c).astype(jnp.float32) + pair_in[n, q, d].astype(jnp.float32)
                near_out[n, step, d] = total.astype(jnp.bfloat16)
                return carry

            lax.fori_loop(0, owners, add, 0)
            sent.append(send(near_out.at[n, step], near_in.at[n, step], s2.at[n, step], r2.at[n, step],
                             replica=q * CORES + c))
        second.append(sent)

    third = {}

    def to_owners(n):
        for copy in second[n]:
            copy.wait_recv()
        third[n] = []
        for step in range(owners):
            d = far_f(step)
            total = mine(n, d, y, c).astype(jnp.float32) + pair_in[n, y, d].astype(jnp.float32)
            for other in range(1, ways):
                total = total + near_in[n, other, d].astype(jnp.float32)
            total = (total * live[n // halves, d].astype(jnp.float32)).astype(jnp.bfloat16)
            if step == 0:
                blocks[n, f, r] = total
            else:
                ready[n, step] = total
                third[n].append(send(ready.at[n, step], blocks.at[n, f, r], s3.at[n, step], r3.at[n, step], fsdp=d))

    fourth = {}

    def to_near(n):
        for copy in third[n]:
            copy.wait_recv()
        fourth[n] = []
        for step in range(1, ways):
            fourth[n].append(send(blocks.at[n, :, r], blocks.at[n, :, r], s4.at[n, step], r4.at[n, step],
                                  replica=far_y(step) * CORES + c))
        fourth[n].append(send(blocks.at[n, :, r], blocks.at[n, :, r], s5.at[n, 0], r5.at[n, 0], replica=mate))

    stored = []

    def to_mate(n):
        last = [fourth[n][-1]]
        for step in range(1, ways):
            fourth[n][step - 1].wait_recv()
            source = lax.rem(y + ways - step, ways) * CORES + c
            last.append(send(blocks.at[n, :, source], blocks.at[n, :, source], s5.at[n, step], r5.at[n, step],
                             replica=mate))
        for copy in last:
            copy.wait_recv()
        keep = pltpu.make_async_copy(blocks.at[n], out.at[n], out_sem.at[n])
        keep.start()
        stored.append(keep)

    for n in range(chunks):
        to_owners(n)
        if n >= 2:
            to_near(n - 2)
    for n in range(max(chunks - 2, 0), chunks):
        to_near(n)
        if n >= 2:
            to_mate(n - 2)
    for n in range(max(chunks - 2, 0), chunks):
        to_mate(n)
    for copy in pending:
        copy.wait_send()
    for keep in stored:
        keep.wait()


def precondition(halves, share, whole, left, right, lroot, rroot, left_out, right_out, update_out):
    r = lax.axis_index("replica")
    size = whole.shape[3]
    part = whole.shape[4]
    scale = (1.0 - decay_rate) / size
    block = jnp.concatenate([whole[0, h, 0] for h in range(halves)], axis=1)
    top = pl.multiple_of(r * share, 16)
    rows = jnp.concatenate([whole[0, h, 0, pl.ds(top, share), :] for h in range(halves)], axis=1)
    lanes = max(share, 128)
    group, shares = lax.div(r, lanes // share), lanes // share
    per = part // lanes
    col_start = pl.multiple_of(lax.rem(group, per) * lanes, 128)
    columns = whole[0, lax.div(group, per), 0, :, pl.ds(col_start, lanes)]
    f32 = jnp.float32
    stat_left = lax.dot_general(rows, block, (((1,), (1,)), ((), ())), preferred_element_type=f32)
    left_out[0, 0] = decay_rate * left[0, 0] + scale * stat_left
    stat_right = lax.dot_general(columns, block, (((0,), (0,)), ((), ())), preferred_element_type=f32)
    mine = stat_right[:share]
    for i in range(1, shares):
        mine = jnp.where(lax.rem(r, shares) == i, stat_right[i * share:(i + 1) * share], mine)
    right_out[0, 0] = decay_rate * right[0, 0] + scale * mine
    half = jnp.dot(lroot[0, 0], block, preferred_element_type=f32).astype(jnp.bfloat16)
    update_out[0, 0] = jnp.dot(half, rroot[0, 0], preferred_element_type=f32).astype(jnp.bfloat16)


def shards(gradients, left_factor, right_factor, left_root, right_root, owner_table):
    owners = lax.axis_size("fsdp")
    replicas = lax.axis_size("replica")
    ways = replicas // CORES
    strip_rows, total_cols = gradients.shape[1:]
    width = left_factor.shape[-1]
    depth, block_rows, share = left_factor.shape[1:4]
    columns = total_cols // width
    per_block = width // strip_rows
    piece = strip_rows // replicas
    halves = HALVES
    part = width // halves
    chunks = depth * halves
    geo = (depth, owners, ways, piece, width, halves, per_block, columns)
    bf16 = jnp.bfloat16
    dma = pltpu.SemaphoreType.DMA
    gathered = pl.pallas_call(
        functools.partial(exchange, geo),
        out_shape=jax.ShapeDtypeStruct((chunks, owners, replicas, piece, part), bf16),
        in_specs=[pl.BlockSpec(memory_space=pltpu.SMEM), pl.BlockSpec(memory_space=pl.ANY)],
        out_specs=pl.BlockSpec(memory_space=pl.ANY),
        scratch_shapes=[
            pltpu.VMEM((columns, strip_rows, width), bf16),
            pltpu.SMEM((depth, owners), jnp.int32),
            pltpu.SMEM((depth, owners), jnp.int32),
            pltpu.VMEM((chunks, ways, owners, piece, part), bf16),
            pltpu.VMEM((chunks, ways, owners, piece, part), bf16),
            pltpu.VMEM((chunks, ways, owners, piece, part), bf16),
            pltpu.VMEM((chunks, ways, owners, piece, part), bf16),
            pltpu.VMEM((chunks, owners, piece, part), bf16),
            pltpu.VMEM((chunks, owners, replicas, piece, part), bf16),
            dma((columns,)),
            dma((chunks,)), dma((chunks,)),
            dma((chunks, ways)), dma((chunks, ways)),
            dma((chunks, owners)), dma((chunks, owners)),
            dma((chunks, ways)), dma((chunks, ways)),
            dma((chunks, ways)), dma((chunks, ways)),
            dma((chunks,)),
        ],
        compiler_params=pltpu.CompilerParams(
            collective_id=0, has_side_effects=True, vmem_limit_bytes=40 * 1024 * 1024
        ),
    )(owner_table, gradients)
    blocks = gathered.reshape(depth, halves, block_rows, width, part)

    def at(k, j):
        return (k, j, 0, 0)

    factor = pl.BlockSpec((1, 1, share, width), at)
    left_new, right_new, update = pl.pallas_call(
        functools.partial(precondition, halves, share),
        grid=(depth, block_rows),
        out_shape=(
            jax.ShapeDtypeStruct(left_factor.shape[1:], jnp.float32),
            jax.ShapeDtypeStruct(left_factor.shape[1:], jnp.float32),
            jax.ShapeDtypeStruct(left_factor.shape[1:], bf16),
        ),
        in_specs=[
            pl.BlockSpec((1, halves, 1, width, part), lambda k, j: (k, 0, j, 0, 0)),
            factor,
            factor,
            factor,
            pl.BlockSpec((1, 1, width, width), at),
        ],
        out_specs=(factor, factor, factor),
        compiler_params=pltpu.CompilerParams(vmem_limit_bytes=32 * 1024 * 1024),
    )(blocks, left_factor[0], right_factor[0], left_root[0], right_root[0])
    return (left_new[None], right_new[None], update[None])


def solution(mesh):
    placed = (
        P("replica", "fsdp", None),
        P("fsdp", None, None, "replica", None),
        P("fsdp", None, None, "replica", None),
        P("fsdp", None, None, "replica", None),
        P("fsdp", None, None, None, None),
        P(),
    )
    factors = P("fsdp", None, None, "replica", None)
    return jax.shard_map(
        shards,
        mesh=mesh,
        in_specs=placed,
        out_specs=(factors, factors, factors),
        check_vma=False,
    )
```

```python
import functools
import math

import jax
import jax.numpy as jnp
from jax import lax
from jax.experimental import pallas as pl
from jax.experimental.pallas import tpu as pltpu
from jax.sharding import PartitionSpec as P

decay_rate = 0.9
MESH = pl.DeviceIdType.MESH
CORES = 2
SUB = 16


def exchange(geo, table, grad, out, owner_of, strip, other, same, cols, live, near_out, near_in, ready,
             table_sem, load_sem, s1, r1, s2, r2, s3, r3, s4, r4, s5, r5, own_sem):
    depth, owners, ways, piece, sub, width, per_block, columns = geo
    chunks = [(k, i) for k in range(depth) for i in range(piece // sub)]
    f = lax.axis_index("fsdp")
    r = lax.axis_index("replica")
    c, y = lax.rem(r, CORES), lax.div(r, CORES)
    mate = y * CORES + (1 - c)
    half = ways * piece

    def far_y(step):
        return lax.rem(y + step, ways)

    def far_f(step):
        return lax.rem(f + step, owners)

    barrier = pltpu.get_barrier_semaphore()
    pl.semaphore_signal(barrier, inc=1, device_id={"replica": mate}, device_id_type=MESH)
    for step in range(1, ways):
        pl.semaphore_signal(barrier, inc=1, device_id={"replica": far_y(step) * CORES + c}, device_id_type=MESH)
    for step in range(1, owners):
        pl.semaphore_signal(barrier, inc=1, device_id={"fsdp": far_f(step)}, device_id_type=MESH)
    names = pltpu.make_async_copy(table, owner_of, table_sem)
    names.start()
    top = pl.multiple_of(c * half, 16)
    for col in range(columns):
        pltpu.make_async_copy(
            grad.at[0, pl.ds(top, half), pl.ds(col * width, width)], strip.at[col], load_sem
        ).start()
    pl.semaphore_wait(barrier, 1 + (ways - 1) + (owners - 1))

    pending = []

    def copy_to(src, dst, s, t, **to):
        return pltpu.make_async_remote_copy(
            src_ref=src, dst_ref=dst, send_sem=s, recv_sem=t, device_id=to, device_id_type=MESH
        )

    def send(src, dst, s, t, **to):
        copy = copy_to(src, dst, s, t, **to)
        copy.start()
        pending.append(copy)
        return copy

    pairs = {}
    for step in list(range(1, ways)) + [0]:
        into = other.at[step - 1] if step else same
        start = pl.multiple_of((1 - c) * half + far_y(step) * piece, 16)
        for col in range(columns):
            copy_to(grad.at[0, pl.ds(start, piece), pl.ds(col * width, width)], into.at[col],
                    s1.at[step], r1.at[step], replica=mate).start()
        pairs[step] = copy_to(into, into, s1.at[step], r1.at[step], replica=mate)
        pending.append(pairs[step])

    names.wait()
    row = lax.div(f, per_block)

    def place(d, carry):
        seen = jnp.int32(0)
        spot = [jnp.int32(0)] * depth
        for col in range(columns):
            hit = owner_of[row, col] == d
            for k in range(depth):
                spot[k] = jnp.where(hit & (seen == k), col, spot[k])
            seen = seen + hit.astype(jnp.int32)
        for k in range(depth):
            cols[k, d] = spot[k]
            live[k, d] = jnp.where(seen > k, 1, 0)
        return carry

    lax.fori_loop(0, owners, place, 0)
    pltpu.make_async_copy(strip, strip, load_sem).wait()

    def pair(n, d, step, kind):
        k, i = chunks[n]
        col = cols[k, d]
        low = pl.multiple_of(far_y(step) * piece + i * sub, 16)
        here = pl.ds(i * sub, sub)
        theirs = other[step - 1, col, here, :] if step else same[col, here, :]
        return strip[col, pl.ds(low, sub), :].astype(kind) + theirs.astype(kind)

    second = [[] for _ in chunks]
    for step in range(1, ways):
        pairs[step].wait_recv()
    for n in range(len(chunks)):
        for step in range(1, ways):
            def add(d, carry):
                near_out[n, step - 1, d] = pair(n, d, step, jnp.bfloat16)
                return carry

            lax.fori_loop(0, owners, add, 0)
            second[n].append(send(near_out.at[n, step - 1], near_in.at[n, step - 1], s2.at[n, step], r2.at[n, step],
                                  replica=far_y(step) * CORES + c))
    pairs[0].wait_recv()

    def rows(n, source):
        k, i = chunks[n]
        spot = lax.rem(source, CORES) * ways + lax.div(source, CORES)
        return out.at[k, :, spot, pl.ds(i * sub, sub)]

    def row_of(n, source):
        k, i = chunks[n]
        spot = lax.rem(source, CORES) * ways + lax.div(source, CORES)
        return out.at[k, f, spot, pl.ds(i * sub, sub)]

    third = {}

    def to_owners(n):
        for copy in second[n]:
            copy.wait_recv()
        third[n] = []
        for step in list(range(1, owners)) + [0]:
            d = far_f(step)
            total = pair(n, d, 0, jnp.float32)
            for other_y in range(1, ways):
                total = total + near_in[n, other_y - 1, d].astype(jnp.float32)
            total = total * live[chunks[n][0], d].astype(jnp.float32)
            ready[n, step] = total.astype(jnp.bfloat16)
            if step == 0:
                own = pltpu.make_async_copy(ready.at[n, 0], row_of(n, r), own_sem.at[n])
                own.start()
                third[n].append(own)
            else:
                third[n].append(send(ready.at[n, step], row_of(n, r), s3.at[n, step], r3.at[n, step], fsdp=d))

    fourth = {}

    def to_near(n):
        third[n][-1].wait()
        for copy in third[n][:-1]:
            copy.wait_recv()
        fourth[n] = []
        for step in range(1, ways):
            fourth[n].append(send(rows(n, r), rows(n, r), s4.at[n, step], r4.at[n, step],
                                  replica=far_y(step) * CORES + c))
        fourth[n].append(send(rows(n, r), rows(n, r), s5.at[n, 0], r5.at[n, 0], replica=mate))

    last = []

    def to_mate(n):
        last.append(fourth[n][-1])
        for step in range(1, ways):
            fourth[n][step - 1].wait_recv()
            source = lax.rem(y + ways - step, ways) * CORES + c
            last.append(send(rows(n, source), rows(n, source), s5.at[n, step], r5.at[n, step], replica=mate))

    count = len(chunks)
    for n in range(count):
        to_owners(n)
        if n >= 2:
            to_near(n - 2)
    for n in range(max(count - 2, 0), count):
        to_near(n)
        if n >= 2:
            to_mate(n - 2)
    for n in range(max(count - 2, 0), count):
        to_mate(n)
    for copy in last:
        copy.wait_recv()
    for copy in pending:
        copy.wait_send()


def precondition(share, whole, left, right, lroot, rroot, left_out, right_out, update_out):
    r = lax.axis_index("replica")
    block = whole[0, 0]
    scale = (1.0 - decay_rate) / block.shape[0]
    rows = whole[0, 0, pl.ds(pl.multiple_of(r * share, 16), share), :]
    lanes = max(share, 128)
    shares = lanes // share
    columns = whole[0, 0, :, pl.ds(pl.multiple_of(lax.div(r, shares) * lanes, 128), lanes)]
    f32 = jnp.float32
    stat_left = lax.dot_general(rows, block, (((1,), (1,)), ((), ())), preferred_element_type=f32)
    left_out[0, 0] = decay_rate * left[0, 0] + scale * stat_left
    stat_right = lax.dot_general(columns, block, (((0,), (0,)), ((), ())), preferred_element_type=f32)
    mine = stat_right[:share]
    for i in range(1, shares):
        mine = jnp.where(lax.rem(r, shares) == i, stat_right[i * share:(i + 1) * share], mine)
    right_out[0, 0] = decay_rate * right[0, 0] + scale * mine
    half = jnp.dot(lroot[0, 0], block, preferred_element_type=f32).astype(jnp.bfloat16)
    update_out[0, 0] = jnp.dot(half, rroot[0, 0], preferred_element_type=f32).astype(jnp.bfloat16)


def shards(gradients, left_factor, right_factor, left_root, right_root, owner_table):
    owners = lax.axis_size("fsdp")
    replicas = lax.axis_size("replica")
    ways = replicas // CORES
    strip_rows, total_cols = gradients.shape[1:]
    width = left_factor.shape[-1]
    depth, block_rows, share = left_factor.shape[1:4]
    columns = total_cols // width
    per_block = width // strip_rows
    piece = strip_rows // replicas
    sub = SUB if piece % SUB == 0 else piece
    chunks = depth * (piece // sub)
    hops = max(ways - 1, 1)
    geo = (depth, owners, ways, piece, sub, width, per_block, columns)
    bf16 = jnp.bfloat16
    dma = pltpu.SemaphoreType.DMA
    buffers = [
        (columns, ways * piece, width),
        (hops, columns, piece, width),
        (columns, piece, width),
        (chunks, hops, owners, sub, width),
        (chunks, hops, owners, sub, width),
        (chunks, owners, sub, width),
    ]
    planned = sum(2 * math.prod(shape) for shape in buffers) + 4 * 1024 * 1024
    vmem = [pltpu.VMEM(shape, bf16) for shape in buffers]
    blocks = pl.pallas_call(
        functools.partial(exchange, geo),
        out_shape=jax.ShapeDtypeStruct((depth, owners, replicas, piece, width), bf16),
        in_specs=[pl.BlockSpec(memory_space=pltpu.HBM), pl.BlockSpec(memory_space=pltpu.HBM)],
        out_specs=pl.BlockSpec(memory_space=pl.ANY),
        scratch_shapes=[
            pltpu.SMEM(owner_table.shape, jnp.int32),
            vmem[0],
            vmem[1],
            vmem[2],
            pltpu.SMEM((depth, owners), jnp.int32),
            pltpu.SMEM((depth, owners), jnp.int32),
            vmem[3],
            vmem[4],
            vmem[5],
            dma, dma,
            dma((ways,)), dma((ways,)),
            dma((chunks, ways)), dma((chunks, ways)),
            dma((chunks, owners)), dma((chunks, owners)),
            dma((chunks, ways)), dma((chunks, ways)),
            dma((chunks, ways)), dma((chunks, ways)),
            dma((chunks,)),
        ],
        compiler_params=pltpu.CompilerParams(collective_id=0, has_side_effects=True, vmem_limit_bytes=planned),
    )(pltpu.with_memory_space_constraint(owner_table, pltpu.HBM),
      pltpu.with_memory_space_constraint(gradients, pltpu.HBM))
    blocks = blocks.reshape(depth, block_rows, width, width)

    def at(k, j):
        return (k, j, 0, 0)

    factor = pl.BlockSpec((1, 1, share, width), at)
    square = pl.BlockSpec((1, 1, width, width), at)
    left_new, right_new, update = pl.pallas_call(
        functools.partial(precondition, share),
        grid=(depth, block_rows),
        out_shape=(
            jax.ShapeDtypeStruct(left_factor.shape[1:], jnp.float32),
            jax.ShapeDtypeStruct(left_factor.shape[1:], jnp.float32),
            jax.ShapeDtypeStruct(left_factor.shape[1:], bf16),
        ),
        in_specs=[square, factor, factor, factor, square],
        out_specs=(factor, factor, factor),
        compiler_params=pltpu.CompilerParams(vmem_limit_bytes=16 * 1024 * 1024),
    )(blocks, left_factor[0], right_factor[0],
      pltpu.with_memory_space_constraint(left_root[0], pltpu.HBM), right_root[0])
    return (left_new[None], right_new[None], update[None])


def solution(mesh):
    placed = (
        P("replica", "fsdp", None),
        P("fsdp", None, None, "replica", None),
        P("fsdp", None, None, "replica", None),
        P("fsdp", None, None, "replica", None),
        P("fsdp", None, None, None, None),
        P(),
    )
    factors = P("fsdp", None, None, "replica", None)
    return jax.shard_map(
        shards,
        mesh=mesh,
        in_specs=placed,
        out_specs=(factors, factors, factors),
        check_vma=False,
    )
```

```python
import functools
import math

import jax
import jax.numpy as jnp
from jax import lax
from jax.experimental import pallas as pl
from jax.experimental.pallas import tpu as pltpu
from jax.sharding import PartitionSpec as P

decay_rate = 0.9
MESH = pl.DeviceIdType.MESH
CORES = 2
SUB = 16


def lanes_of(share, r):
    lanes = max(share, 128)
    return pl.ds(pl.multiple_of(lax.div(r, lanes // share) * lanes, 128), lanes)


def products(share, r, whole, rows, columns, left, right, lroot, rroot):
    scale = (1.0 - decay_rate) / whole.shape[0]
    shares = columns.shape[1] // share
    f32 = jnp.float32
    stat_left = lax.dot_general(rows, whole, (((1,), (1,)), ((), ())), preferred_element_type=f32)
    left_new = decay_rate * left[...] + scale * stat_left
    stat_right = lax.dot_general(columns, whole, (((0,), (0,)), ((), ())), preferred_element_type=f32)
    mine = stat_right[:share]
    for i in range(1, shares):
        mine = jnp.where(lax.rem(r, shares) == i, stat_right[i * share:(i + 1) * share], mine)
    right_new = decay_rate * right[...] + scale * mine
    half = jnp.dot(lroot[...], whole, preferred_element_type=f32).astype(jnp.bfloat16)
    update = jnp.dot(half, rroot[...], preferred_element_type=f32).astype(jnp.bfloat16)
    return left_new, right_new, update


def exchange(geo, table, grad, *refs):
    (depth, owners, ways, piece, sub, width, per_block, columns, share) = geo
    early = depth - 1
    refs = list(refs)
    given = [refs.pop(0) for _ in range(4)]
    out, kept = refs.pop(0), refs.pop(0)
    done = [refs.pop(0) for _ in range(3)] if early else []
    held = [refs.pop(0) for _ in range(6)] if early else []
    early_in, early_out, block_sem = (refs.pop(0) for _ in range(3))
    _exchange(geo, table, grad, given, out, kept, done, held, early_in, early_out, block_sem, *refs)


def _exchange(geo, table, grad, given, out, kept, done, held, early_in, early_out, block_sem, owner_of, strip, other, same, cols, live, near_out, near_in, ready,
             table_sem, load_sem, s1, r1, s2, r2, s3, r3, s4, r4, s5, r5, own_sem):
    depth, owners, ways, piece, sub, width, per_block, columns, share = geo
    early = depth - 1
    subs = piece // sub
    chunks = [(k, i) for k in range(depth) for i in range(subs)]
    f = lax.axis_index("fsdp")
    r = lax.axis_index("replica")
    c, y = lax.rem(r, CORES), lax.div(r, CORES)
    mate = y * CORES + (1 - c)
    half = ways * piece

    def far_y(step):
        return lax.rem(y + step, ways)

    def far_f(step):
        return lax.rem(f + step, owners)

    barrier = pltpu.get_barrier_semaphore()
    pl.semaphore_signal(barrier, inc=1, device_id={"replica": mate}, device_id_type=MESH)
    for step in range(1, ways):
        pl.semaphore_signal(barrier, inc=1, device_id={"replica": far_y(step) * CORES + c}, device_id_type=MESH)
    for step in range(1, owners):
        pl.semaphore_signal(barrier, inc=1, device_id={"fsdp": far_f(step)}, device_id_type=MESH)
    names = pltpu.make_async_copy(table, owner_of, table_sem)
    names.start()
    top = pl.multiple_of(c * half, 16)
    for col in range(columns):
        pltpu.make_async_copy(
            grad.at[0, pl.ds(top, half), pl.ds(col * width, width)], strip.at[col], load_sem
        ).start()
    pl.semaphore_wait(barrier, 1 + (ways - 1) + (owners - 1))

    pending = []

    def copy_to(src, dst, s, t, **to):
        return pltpu.make_async_remote_copy(
            src_ref=src, dst_ref=dst, send_sem=s, recv_sem=t, device_id=to, device_id_type=MESH
        )

    def send(src, dst, s, t, **to):
        copy = copy_to(src, dst, s, t, **to)
        copy.start()
        pending.append(copy)
        return copy

    pairs = {}

    def to_pair(step):
        into = other.at[step - 1] if step else same
        start = pl.multiple_of((1 - c) * half + far_y(step) * piece, 16)
        for col in range(columns):
            copy_to(grad.at[0, pl.ds(start, piece), pl.ds(col * width, width)], into.at[col],
                    s1.at[step], r1.at[step], replica=mate).start()
        pairs[step] = copy_to(into, into, s1.at[step], r1.at[step], replica=mate)
        pending.append(pairs[step])

    for step in range(1, ways):
        to_pair(step)
    names.wait()
    row = lax.div(f, per_block)

    def place(d, carry):
        seen = jnp.int32(0)
        spot = [jnp.int32(0)] * depth
        for col in range(columns):
            hit = owner_of[row, col] == d
            for k in range(depth):
                spot[k] = jnp.where(hit & (seen == k), col, spot[k])
            seen = seen + hit.astype(jnp.int32)
        for k in range(depth):
            cols[k, d] = spot[k]
            live[k, d] = jnp.where(seen > k, 1, 0)
        return carry

    lax.fori_loop(0, owners, place, 0)
    pltpu.make_async_copy(strip, strip, load_sem).wait()

    def pair(n, d, step, kind):
        k, i = chunks[n]
        col = cols[k, d]
        low = pl.multiple_of(far_y(step) * piece + i * sub, 16)
        here = pl.ds(i * sub, sub)
        theirs = other[step - 1, col, here, :] if step else same[col, here, :]
        return strip[col, pl.ds(low, sub), :].astype(kind) + theirs.astype(kind)

    second = {}

    def to_far(n):
        second[n] = []
        for step in range(1, ways):
            def add(d, carry):
                near_out[n, step - 1, d] = pair(n, d, step, jnp.bfloat16)
                return carry

            lax.fori_loop(0, owners, add, 0)
            second[n].append(send(near_out.at[n, step - 1], near_in.at[n, step - 1], s2.at[n, step], r2.at[n, step],
                                  replica=far_y(step) * CORES + c))

    for step in range(1, ways):
        pairs[step].wait_recv()
    to_far(0)
    to_pair(0)
    loads = [pltpu.make_async_copy(given[2].at[depth - 1], kept, early_in.at[0])]
    for i in range(4 if early else 0):
        loads.append(pltpu.make_async_copy(given[i].at[pl.ds(0, early)], held[i], early_in.at[i + 1]))
    for load in loads:
        load.start()
    if len(chunks) > 1:
        to_far(1)
    pairs[0].wait_recv()

    def rows(n, source):
        k, i = chunks[n]
        spot = lax.rem(source, CORES) * ways + lax.div(source, CORES)
        return out.at[k, :, spot, pl.ds(i * sub, sub)]

    def row_of(n, source):
        k, i = chunks[n]
        spot = lax.rem(source, CORES) * ways + lax.div(source, CORES)
        return out.at[k, f, spot, pl.ds(i * sub, sub)]

    third = {}

    def to_owners(n):
        for copy in second[n]:
            copy.wait_recv()
        third[n] = []
        for step in list(range(1, owners)) + [0]:
            d = far_f(step)
            total = pair(n, d, 0, jnp.float32)
            for other_y in range(1, ways):
                total = total + near_in[n, other_y - 1, d].astype(jnp.float32)
            total = total * live[chunks[n][0], d].astype(jnp.float32)
            ready[n, step] = total.astype(jnp.bfloat16)
            if step == 0:
                own = pltpu.make_async_copy(ready.at[n, 0], row_of(n, r), own_sem.at[n])
                own.start()
                third[n].append(own)
            else:
                third[n].append(send(ready.at[n, step], row_of(n, r), s3.at[n, step], r3.at[n, step], fsdp=d))

    fourth = {}

    def to_near(n):
        third[n][-1].wait()
        for copy in third[n][:-1]:
            copy.wait_recv()
        fourth[n] = []
        for step in range(1, ways):
            fourth[n].append(send(rows(n, r), rows(n, r), s4.at[n, step], r4.at[n, step],
                                  replica=far_y(step) * CORES + c))
        fourth[n].append(send(rows(n, r), rows(n, r), s5.at[n, 0], r5.at[n, 0], replica=mate))

    last = {}

    def to_mate(n):
        last[n] = [fourth[n][-1]]
        for step in range(1, ways):
            fourth[n][step - 1].wait_recv()
            source = lax.rem(y + ways - step, ways) * CORES + c
            last[n].append(send(rows(n, source), rows(n, source), s5.at[n, step], r5.at[n, step], replica=mate))

    def multiply(k):
        for n in range(k * subs, (k + 1) * subs):
            for copy in last.pop(n):
                copy.wait_recv()
        left, right, lroot, rroot, update, block = held
        fetch = pltpu.make_async_copy(out.at[k], block.at[k], block_sem.at[k])
        fetch.start()
        if k == 0:
            for load in loads[1:]:
                load.wait()
        fetch.wait()
        for j in range(owners // per_block):
            strips = pl.ds(j * per_block, per_block)
            whole = block[k, strips].reshape(width, width)
            columns_mine = block[k, strips, :, :, lanes_of(share, r)].reshape(width, -1)
            strip_rows = ways * CORES * piece
            if share % strip_rows == 0:
                held_rows = block[k, pl.ds(j * per_block + r * (share // strip_rows), share // strip_rows)]
            else:
                first_piece = lax.div(lax.rem(r * share, strip_rows), piece)
                held_rows = block[k, j * per_block + lax.div(r * share, strip_rows), pl.ds(first_piece, share // piece)]
            value = products(share, r, whole, held_rows.reshape(share, width), columns_mine,
                             left.at[k, j], right.at[k, j], lroot.at[k, j], rroot.at[k, j])
            left[k, j], right[k, j], update[k, j] = value
        stores = []
        for i, source in enumerate((left, right, update)):
            stores.append(pltpu.make_async_copy(source.at[k], done[i].at[k], early_out.at[k, i]))
            stores[-1].start()
        return stores

    count = len(chunks)
    for n in range(count):
        to_owners(n)
        if n + 2 < count:
            to_far(n + 2)
        if n >= 2:
            to_near(n - 2)
    late = list(range(count))
    if count > 2:
        to_mate(late.pop(0))
    for n in range(max(count - 2, 0), count):
        to_near(n)
    stores = []
    for n in late:
        to_mate(n)
        k = n // subs
        if k < early and n == (k + 1) * subs - 1:
            stores += multiply(k)
    for copies in last.values():
        for copy in copies:
            copy.wait_recv()
    for copy in pending:
        copy.wait_send()
    loads[0].wait()
    for store in stores:
        store.wait()


def precondition(early, share, *refs):
    refs = list(refs)
    blocks, left, right, lroot, rroot = (refs.pop(0) for _ in range(5))
    ready = [refs.pop(0) for _ in range(3)] if early else []
    outs = [refs.pop(0) for _ in range(3)]
    block, mine, answer = refs.pop(0), [refs.pop(0) for _ in range(4)], refs.pop(0)
    in_sem, ready_sem, out_sem = refs
    r = lax.axis_index("replica")
    count = block.shape[0]
    fetches = []
    for j in range(count):
        sources = [blocks.at[early, j], left.at[early, j], right.at[early, j], lroot.at[j], rroot.at[early, j]]
        fetches.append([pltpu.make_async_copy(source, target.at[j], in_sem.at[j, i])
                        for i, (source, target) in enumerate(zip(sources, [block] + mine))])
        for fetch in fetches[-1]:
            fetch.start()
    stores = []
    for i, source in enumerate(ready):
        stores.append(pltpu.make_async_copy(source, outs[i].at[pl.ds(0, early)], ready_sem.at[i]))
        stores[-1].start()
    for j in range(count):
        for fetch in fetches[j]:
            fetch.wait()
        rows = block[j, pl.ds(pl.multiple_of(r * share, 16), share), :]
        values = products(share, r, block[j], rows, block[j, :, lanes_of(share, r)], *(ref.at[j] for ref in mine))
        targets = (mine[0], mine[1], answer)
        for i in range(3):
            targets[i][j] = values[i]
            stores.append(pltpu.make_async_copy(targets[i].at[j], outs[i].at[early, j], out_sem.at[j, i]))
            stores[-1].start()
    for store in stores:
        store.wait()


def shards(gradients, left_factor, right_factor, left_root, right_root, owner_table):
    owners = lax.axis_size("fsdp")
    replicas = lax.axis_size("replica")
    ways = replicas // CORES
    strip_rows, total_cols = gradients.shape[1:]
    width = left_factor.shape[-1]
    depth, block_rows, share = left_factor.shape[1:4]
    columns = total_cols // width
    per_block = width // strip_rows
    piece = strip_rows // replicas
    sub = SUB if piece % SUB == 0 else piece
    chunks = depth * (piece // sub)
    hops = max(ways - 1, 1)
    geo = (depth, owners, ways, piece, sub, width, per_block, columns, share)
    early = depth - 1
    bf16 = jnp.bfloat16
    dma = pltpu.SemaphoreType.DMA
    buffers = [
        (columns, ways * piece, width),
        (hops, columns, piece, width),
        (columns, piece, width),
        (chunks, hops, owners, sub, width),
        (chunks, hops, owners, sub, width),
        (chunks, owners, sub, width),
    ]
    vmem = [pltpu.VMEM(shape, bf16) for shape in buffers]
    f32 = jnp.float32

    def parts(count):
        return [(count, block_rows, share, width)] * 3 + [(count, block_rows, width, width)]

    held = []
    if early:
        shapes = parts(early)
        held = [pltpu.VMEM(shape, kind) for shape, kind in zip(shapes, (f32, f32, bf16, bf16))]
        held += [pltpu.VMEM(shapes[0], bf16), pltpu.VMEM((early, owners, replicas, piece, width), bf16)]
    planned = sum(math.prod(ref.shape) * jnp.dtype(ref.dtype).itemsize for ref in vmem + held) + 6 * 1024 * 1024
    given = [left_factor[0], right_factor[0], left_root[0], right_root[0]]
    result = parts(depth)[0]
    anywhere = pl.BlockSpec(memory_space=pl.ANY)
    first = [jax.ShapeDtypeStruct((depth, owners, replicas, piece, width), bf16),
             jax.ShapeDtypeStruct(result[1:], bf16)]
    if early:
        first += [jax.ShapeDtypeStruct((early,) + result[1:], kind) for kind in (f32, f32, bf16)]
    blocks, lroot, *ready = pl.pallas_call(
        functools.partial(exchange, geo),
        out_shape=tuple(first),
        in_specs=[pl.BlockSpec(memory_space=pltpu.HBM)] * 6,
        out_specs=(anywhere,) * len(first),
        scratch_shapes=held + [
            dma((5,)), dma((max(early, 1), 3)), dma((max(early, 1),)),
            pltpu.SMEM(owner_table.shape, jnp.int32),
            vmem[0],
            vmem[1],
            vmem[2],
            pltpu.SMEM((depth, owners), jnp.int32),
            pltpu.SMEM((depth, owners), jnp.int32),
            vmem[3],
            vmem[4],
            vmem[5],
            dma, dma,
            dma((ways,)), dma((ways,)),
            dma((chunks, ways)), dma((chunks, ways)),
            dma((chunks, owners)), dma((chunks, owners)),
            dma((chunks, ways)), dma((chunks, ways)),
            dma((chunks, ways)), dma((chunks, ways)),
            dma((chunks,)),
        ],
        compiler_params=pltpu.CompilerParams(collective_id=0, has_side_effects=True, vmem_limit_bytes=planned),
    )(*(pltpu.with_memory_space_constraint(x, pltpu.HBM) for x in [owner_table, gradients] + given))
    blocks = blocks.reshape(depth, block_rows, width, width)

    shapes = parts(1)
    outs = (jax.ShapeDtypeStruct(result, f32), jax.ShapeDtypeStruct(result, f32), jax.ShapeDtypeStruct(result, bf16))
    results = pl.pallas_call(
        functools.partial(precondition, early, share),
        out_shape=outs,
        in_specs=[anywhere] * (5 + len(ready)),
        out_specs=(anywhere,) * 3,
        scratch_shapes=[
            pltpu.VMEM((block_rows, width, width), bf16),
            pltpu.VMEM(shapes[0][1:], f32),
            pltpu.VMEM(shapes[0][1:], f32),
            pltpu.VMEM(shapes[0][1:], bf16),
            pltpu.VMEM(shapes[3][1:], bf16),
            pltpu.VMEM(shapes[0][1:], bf16),
            dma((block_rows, 5)), dma((3,)), dma((block_rows, 3)),
        ],
        compiler_params=pltpu.CompilerParams(vmem_limit_bytes=20 * 1024 * 1024),
    )(blocks, given[0], given[1], lroot, given[3], *ready)
    return tuple(x[None] for x in results)


def solution(mesh):
    placed = (
        P("replica", "fsdp", None),
        P("fsdp", None, None, "replica", None),
        P("fsdp", None, None, "replica", None),
        P("fsdp", None, None, "replica", None),
        P("fsdp", None, None, None, None),
        P(),
    )
    factors = P("fsdp", None, None, "replica", None)
    return jax.shard_map(
        shards,
        mesh=mesh,
        in_specs=placed,
        out_specs=(factors, factors, factors),
        check_vma=False,
    )
```

```python
import functools
import math

import jax
import jax.numpy as jnp
from jax import lax
from jax.experimental import pallas as pl
from jax.experimental.pallas import tpu as pltpu
from jax.sharding import PartitionSpec as P

decay_rate = 0.9
MESH = pl.DeviceIdType.MESH
CORES = 2
SUB = 16


def lanes_of(share, r):
    lanes = max(share, 128)
    return pl.ds(pl.multiple_of(lax.div(r, lanes // share) * lanes, 128), lanes)


def products(share, r, whole, rows, columns, left, right, lroot, rroot):
    scale = (1.0 - decay_rate) / whole.shape[0]
    shares = columns.shape[1] // share
    f32 = jnp.float32
    stat_left = lax.dot_general(rows, whole, (((1,), (1,)), ((), ())), preferred_element_type=f32)
    left_new = decay_rate * left[...] + scale * stat_left
    stat_right = lax.dot_general(columns, whole, (((0,), (0,)), ((), ())), preferred_element_type=f32)
    mine = stat_right[:share]
    for i in range(1, shares):
        mine = jnp.where(lax.rem(r, shares) == i, stat_right[i * share:(i + 1) * share], mine)
    right_new = decay_rate * right[...] + scale * mine
    half = jnp.dot(lroot[...], whole, preferred_element_type=f32).astype(jnp.bfloat16)
    update = jnp.dot(half, rroot[...], preferred_element_type=f32).astype(jnp.bfloat16)
    return left_new, right_new, update


def exchange(geo, table, grad, *refs):
    refs = list(refs)
    given = [refs.pop(0) for _ in range(4)]
    out, kept = refs.pop(0), refs.pop(0)
    done = [refs.pop(0) for _ in range(3)] if geo[-1] else []
    held = [refs.pop(0) for _ in range(6)] if geo[-1] else []
    early_in, early_out, block_sem = (refs.pop(0) for _ in range(3))
    _exchange(geo, table, grad, given, out, kept, done, held, early_in, early_out, block_sem, *refs)


def _exchange(geo, table, grad, given, out, kept, done, held, early_in, early_out, block_sem,
              owner_of, strip, other, same, pair_far, pair_same, cols, live, near_out, near_in, ready,
              table_sem, load_sem, s1, r1, s2, r2, s3, r3, s4, r4, s5, r5, own_sem):
    depth, owners, ways, piece, sub, width, per_block, columns, share, early = geo
    subs = piece // sub
    chunks = [(k, i) for k in range(depth) for i in range(subs)]
    f = lax.axis_index("fsdp")
    r = lax.axis_index("replica")
    c, y = lax.rem(r, CORES), lax.div(r, CORES)
    mate = y * CORES + (1 - c)
    half = ways * piece

    def far_y(step):
        return lax.rem(y + step, ways)

    def far_f(step):
        return lax.rem(f + step, owners)

    barrier = pltpu.get_barrier_semaphore()
    pl.semaphore_signal(barrier, inc=1, device_id={"replica": mate}, device_id_type=MESH)
    for step in range(1, ways):
        pl.semaphore_signal(barrier, inc=1, device_id={"replica": far_y(step) * CORES + c}, device_id_type=MESH)
    for step in range(1, owners):
        pl.semaphore_signal(barrier, inc=1, device_id={"fsdp": far_f(step)}, device_id_type=MESH)
    names = pltpu.make_async_copy(table, owner_of, table_sem)
    names.start()
    pl.semaphore_wait(barrier, 1 + (ways - 1) + (owners - 1))

    pending = []

    def copy_to(src, dst, s, t, **to):
        return pltpu.make_async_remote_copy(
            src_ref=src, dst_ref=dst, send_sem=s, recv_sem=t, device_id=to, device_id_type=MESH
        )

    def send(src, dst, s, t, **to):
        copy = copy_to(src, dst, s, t, **to)
        copy.start()
        pending.append(copy)
        return copy

    pairs = {}

    def to_pair(step, i):
        into = other.at[step - 1, pl.ds(i * sub, sub)] if step else same.at[pl.ds(i * sub, sub)]
        start = pl.multiple_of((1 - c) * half + far_y(step) * piece + i * sub, 16)
        pairs[step, i] = send(grad.at[0, pl.ds(start, sub)], into, s1.at[step, i], r1.at[step, i], replica=mate)

    def near_rows(step):
        return pl.ds(pl.multiple_of(far_y(step) * piece, 16), piece)

    mine = {}
    for step in list(range(1, ways)) + [0]:
        for i in range(subs if step else 0):
            to_pair(step, i)
        start = pl.multiple_of(c * half + far_y(step) * piece, 16)
        mine[step] = pltpu.make_async_copy(grad.at[0, pl.ds(start, piece)], strip.at[near_rows(step)], load_sem.at[step])
        mine[step].start()
    names.wait()
    row = lax.div(f, per_block)

    def place(d, carry):
        seen = jnp.int32(0)
        spot = [jnp.int32(0)] * depth
        for col in range(columns):
            hit = owner_of[row, col] == d
            for k in range(depth):
                spot[k] = jnp.where(hit & (seen == k), col, spot[k])
            seen = seen + hit.astype(jnp.int32)
        for k in range(depth):
            cols[k, d] = spot[k]
            live[k, d] = jnp.where(seen > k, 1, 0)
        return carry

    lax.fori_loop(0, owners, place, 0)

    def pair(step, i):
        pairs[step, i].wait_recv()
        low = pl.multiple_of(far_y(step) * piece + i * sub, 16)
        here = pl.ds(i * sub, sub)

        def add(col, carry):
            lanes = pl.ds(pl.multiple_of(col * width, 128), width)
            theirs = other[step - 1, here, lanes] if step else same[here, lanes]
            total = strip[pl.ds(low, sub), lanes].astype(jnp.float32) + theirs.astype(jnp.float32)
            if step:
                pair_far[step - 1, col, here, :] = total.astype(jnp.bfloat16)
            else:
                pair_same[col, here, :] = total
            return carry

        lax.fori_loop(0, columns, add, 0)

    second = {}

    def to_far(n):
        second[n] = []
        k, i = chunks[n]
        for step in range(1, ways):
            if k == 0:
                if i == 0:
                    mine[step].wait()
                pair(step, i)

            def pick(d, carry):
                near_out[n, step - 1, d] = pair_far[step - 1, cols[k, d], i * sub:(i + 1) * sub, :]
                return carry

            lax.fori_loop(0, owners, pick, 0)
            second[n].append(send(near_out.at[n, step - 1], near_in.at[n, step - 1], s2.at[n, step], r2.at[n, step],
                                  replica=far_y(step) * CORES + c))

    to_far(0)
    for i in range(subs):
        to_pair(0, i)
    if len(chunks) > 1:
        to_far(1)
    loads = [pltpu.make_async_copy(given[2].at[early], kept, early_in.at[0])]
    for i in range(4 if early else 0):
        loads.append(pltpu.make_async_copy(given[i].at[pl.ds(0, early)], held[i], early_in.at[i + 1]))
    for load in loads:
        load.start()
    mine[0].wait()
    for i in range(subs):
        pair(0, i)

    block_rows = owners // per_block

    def rows(m, source):
        k, j = m // block_rows, m % block_rows
        spot = lax.rem(source, CORES) * ways + lax.div(source, CORES)
        return out.at[k, pl.ds(j * per_block, per_block), spot]

    def row_of(n, source):
        k, i = chunks[n]
        spot = lax.rem(source, CORES) * ways + lax.div(source, CORES)
        return out.at[k, f, spot, pl.ds(i * sub, sub)]

    third = {}

    def to_owners(n):
        for copy in second[n]:
            copy.wait_recv()
        third[n] = []
        for step in list(range(1, owners)) + [0]:
            d = far_f(step)
            k, i = chunks[n]
            total = pair_same[cols[k, d], i * sub:(i + 1) * sub, :]
            for other_y in range(1, ways):
                total = total + near_in[n, other_y - 1, d].astype(jnp.float32)
            total = total * live[chunks[n][0], d].astype(jnp.float32)
            ready[n, step] = total.astype(jnp.bfloat16)
            if step == 0:
                own = pltpu.make_async_copy(ready.at[n, 0], row_of(n, r), own_sem.at[n])
                own.start()
                third[n].append(own)
            else:
                third[n].append(send(ready.at[n, step], row_of(n, r), s3.at[n, step], r3.at[n, step], fsdp=d))

    fourth = {}

    def to_near(k):
        for n in range(k * subs, (k + 1) * subs):
            third[n][-1].wait()
            for copy in third[n][:-1]:
                copy.wait_recv()
        for m in range(k * block_rows, (k + 1) * block_rows):
            fourth[m] = []
            for step in range(1, ways):
                fourth[m].append(send(rows(m, r), rows(m, r), s4.at[m, step], r4.at[m, step],
                                      replica=far_y(step) * CORES + c))
            fourth[m].append(send(rows(m, r), rows(m, r), s5.at[m, 0], r5.at[m, 0], replica=mate))

    last = {}

    def to_mate(n):
        last[n] = [fourth[n][-1]]
        for step in range(1, ways):
            fourth[n][step - 1].wait_recv()
            source = lax.rem(y + ways - step, ways) * CORES + c
            last[n].append(send(rows(n, source), rows(n, source), s5.at[n, step], r5.at[n, step], replica=mate))

    def multiply(m):
        k, j = m // block_rows, m % block_rows
        for copy in last.pop(m):
            copy.wait_recv()
        left, right, lroot, rroot, update, block = held
        fetch = pltpu.make_async_copy(out.at[k, pl.ds(j * per_block, per_block)], block.at[m], block_sem.at[m])
        fetch.start()
        if m == 0:
            for load in loads[1:]:
                load.wait()
        fetch.wait()
        whole = block[m].reshape(width, width)
        columns_mine = block[m, :, :, :, lanes_of(share, r)].reshape(width, -1)
        strip_rows = ways * CORES * piece
        if share % strip_rows == 0:
            held_rows = block[m, pl.ds(r * (share // strip_rows), share // strip_rows)]
        else:
            first_piece = lax.div(lax.rem(r * share, strip_rows), piece)
            held_rows = block[m, lax.div(r * share, strip_rows), pl.ds(first_piece, share // piece)]
        value = products(share, r, whole, held_rows.reshape(share, width), columns_mine,
                         left.at[m], right.at[m], lroot.at[m], rroot.at[m])
        left[m], right[m], update[m] = value
        for i, source in enumerate((left, right, update)):
            stores.append(pltpu.make_async_copy(source.at[m], done[i].at[m], early_out.at[m, i]))
            stores[-1].start()

    stores = []
    count = len(chunks)
    for n in range(count):
        to_owners(n)
        if n + 2 < count:
            to_far(n + 2)
        if n >= subs and n % subs == 0:
            to_near(n // subs - 1)
    to_near(depth - 1)
    for m in range(early + 1):
        to_mate(m)
        if m < early:
            multiply(m)
    for copies in last.values():
        for copy in copies:
            copy.wait_recv()
    for copy in pending:
        copy.wait_send()
    loads[0].wait()
    for store in stores:
        store.wait()


def precondition(early, share, *refs):
    refs = list(refs)
    blocks, left, right, lroot, rroot = (refs.pop(0) for _ in range(5))
    ready = [refs.pop(0) for _ in range(3)] if early else []
    outs = [refs.pop(0) for _ in range(3)]
    block, mine, answer = refs.pop(0), [refs.pop(0) for _ in range(4)], refs.pop(0)
    in_sem, ready_sem, out_sem = refs
    r = lax.axis_index("replica")
    sources = [blocks.at[early], left.at[early], right.at[early], lroot, rroot.at[early]]
    fetches = [pltpu.make_async_copy(source, target, in_sem.at[i])
               for i, (source, target) in enumerate(zip(sources, [block] + mine))]
    for fetch in fetches:
        fetch.start()
    stores = []
    for i, source in enumerate(ready):
        stores.append(pltpu.make_async_copy(source, outs[i].at[pl.ds(0, early)], ready_sem.at[i]))
        stores[-1].start()
    for fetch in fetches:
        fetch.wait()
    rows = block[pl.ds(pl.multiple_of(r * share, 16), share), :]
    values = products(share, r, block[...], rows, block[:, lanes_of(share, r)], *mine)
    for i, target in enumerate((mine[0], mine[1], answer)):
        target[...] = values[i]
        stores.append(pltpu.make_async_copy(target, outs[i].at[early], out_sem.at[i]))
        stores[-1].start()
    for store in stores:
        store.wait()


def shards(gradients, left_factor, right_factor, left_root, right_root, owner_table):
    owners = lax.axis_size("fsdp")
    replicas = lax.axis_size("replica")
    ways = replicas // CORES
    strip_rows, total_cols = gradients.shape[1:]
    width = left_factor.shape[-1]
    depth, block_rows, share = left_factor.shape[1:4]
    columns = total_cols // width
    per_block = width // strip_rows
    piece = strip_rows // replicas
    sub = SUB if piece % SUB == 0 else piece
    chunks = depth * (piece // sub)
    hops = max(ways - 1, 1)
    total = depth * block_rows
    early = total - 1
    geo = (depth, owners, ways, piece, sub, width, per_block, columns, share, early)
    bf16 = jnp.bfloat16
    dma = pltpu.SemaphoreType.DMA
    vmem = [pltpu.VMEM(shape, kind) for shape, kind in (
        ((ways * piece, total_cols), bf16),
        ((hops, piece, total_cols), bf16),
        ((piece, total_cols), bf16),
        ((hops, columns, piece, width), bf16),
        ((columns, piece, width), jnp.float32),
        ((chunks, hops, owners, sub, width), bf16),
        ((chunks, hops, owners, sub, width), bf16),
        ((chunks, owners, sub, width), bf16),
    )]
    f32 = jnp.float32

    def parts(count):
        return [(count, share, width)] * 3 + [(count, width, width)]

    held = []
    if early:
        shapes = parts(early)
        held = [pltpu.VMEM(shape, kind) for shape, kind in zip(shapes, (f32, f32, bf16, bf16))]
        held += [pltpu.VMEM(shapes[0], bf16), pltpu.VMEM((early, per_block, replicas, piece, width), bf16)]
    planned = sum(math.prod(ref.shape) * jnp.dtype(ref.dtype).itemsize for ref in vmem + held) + 6 * 1024 * 1024
    given = [x.reshape(shape) for x, shape in
             zip((left_factor, right_factor, left_root, right_root), parts(total))]
    result = parts(total)[0]
    anywhere = pl.BlockSpec(memory_space=pl.ANY)
    first = [jax.ShapeDtypeStruct((depth, owners, replicas, piece, width), bf16),
             jax.ShapeDtypeStruct(result[1:], bf16)]
    if early:
        first += [jax.ShapeDtypeStruct((early,) + result[1:], kind) for kind in (f32, f32, bf16)]
    blocks, lroot, *ready = pl.pallas_call(
        functools.partial(exchange, geo),
        out_shape=tuple(first),
        in_specs=[pl.BlockSpec(memory_space=pltpu.HBM)] * 6,
        out_specs=(anywhere,) * len(first),
        scratch_shapes=held + [
            dma((5,)), dma((total, 3)), dma((total,)),
            pltpu.SMEM(owner_table.shape, jnp.int32),
            *vmem[:5],
            pltpu.SMEM((depth, owners), jnp.int32),
            pltpu.SMEM((depth, owners), jnp.int32),
            *vmem[5:],
            dma, dma((ways,)),
            dma((ways, piece // sub)), dma((ways, piece // sub)),
            dma((chunks, ways)), dma((chunks, ways)),
            dma((chunks, owners)), dma((chunks, owners)),
            dma((total, ways)), dma((total, ways)),
            dma((total, ways)), dma((total, ways)),
            dma((chunks,)),
        ],
        compiler_params=pltpu.CompilerParams(collective_id=0, has_side_effects=True, vmem_limit_bytes=planned),
    )(*(pltpu.with_memory_space_constraint(x, pltpu.HBM) for x in [owner_table, gradients] + given))
    blocks = blocks.reshape(total, width, width)

    shapes = parts(1)
    outs = (jax.ShapeDtypeStruct(result, f32), jax.ShapeDtypeStruct(result, f32), jax.ShapeDtypeStruct(result, bf16))
    results = pl.pallas_call(
        functools.partial(precondition, early, share),
        out_shape=outs,
        in_specs=[anywhere] * (5 + len(ready)),
        out_specs=(anywhere,) * 3,
        scratch_shapes=[
            pltpu.VMEM((width, width), bf16),
            pltpu.VMEM(shapes[0][1:], f32),
            pltpu.VMEM(shapes[0][1:], f32),
            pltpu.VMEM(shapes[0][1:], bf16),
            pltpu.VMEM(shapes[3][1:], bf16),
            pltpu.VMEM(shapes[0][1:], bf16),
            dma((5,)), dma((3,)), dma((3,)),
        ],
        compiler_params=pltpu.CompilerParams(vmem_limit_bytes=20 * 1024 * 1024),
    )(blocks, given[0], given[1], lroot, given[3], *ready)
    return tuple(x.reshape(left_factor.shape) for x in results)


def solution(mesh):
    placed = (
        P("replica", "fsdp", None),
        P("fsdp", None, None, "replica", None),
        P("fsdp", None, None, "replica", None),
        P("fsdp", None, None, "replica", None),
        P("fsdp", None, None, None, None),
        P(),
    )
    factors = P("fsdp", None, None, "replica", None)
    return jax.shard_map(
        shards,
        mesh=mesh,
        in_specs=placed,
        out_specs=(factors, factors, factors),
        check_vma=False,
    )
```

```python
import functools
import math

import jax
import jax.numpy as jnp
from jax import lax
from jax.experimental import pallas as pl
from jax.experimental.pallas import tpu as pltpu
from jax.sharding import PartitionSpec as P

decay_rate = 0.9
MESH = pl.DeviceIdType.MESH
CORES = 2
SUB = 16


def lanes_of(share, r):
    lanes = max(share, 128)
    return pl.ds(pl.multiple_of(lax.div(r, lanes // share) * lanes, 128), lanes)


def products(share, r, whole, rows, columns, left, right, lroot, rroot):
    scale = (1.0 - decay_rate) / whole.shape[0]
    shares = columns.shape[1] // share
    f32 = jnp.float32
    stat_left = lax.dot_general(rows, whole, (((1,), (1,)), ((), ())), preferred_element_type=f32)
    left_new = decay_rate * left[...] + scale * stat_left
    stat_right = lax.dot_general(columns, whole, (((0,), (0,)), ((), ())), preferred_element_type=f32)
    mine = stat_right[:share]
    for i in range(1, shares):
        mine = jnp.where(lax.rem(r, shares) == i, stat_right[i * share:(i + 1) * share], mine)
    right_new = decay_rate * right[...] + scale * mine
    half = jnp.dot(lroot[...], whole, preferred_element_type=f32).astype(jnp.bfloat16)
    update = jnp.dot(half, rroot[...], preferred_element_type=f32).astype(jnp.bfloat16)
    return left_new, right_new, update


def exchange(geo, table, grad, *refs):
    refs = list(refs)
    given = [refs.pop(0) for _ in range(4)]
    out, kept = refs.pop(0), refs.pop(0)
    done = [refs.pop(0) for _ in range(3)] if geo[-1] else []
    held = [refs.pop(0) for _ in range(6)] if geo[-1] else []
    early_in, early_out, block_sem = (refs.pop(0) for _ in range(3))
    _exchange(geo, table, grad, given, out, kept, done, held, early_in, early_out, block_sem, *refs)


def _exchange(geo, table, grad, given, out, kept, done, held, early_in, early_out, block_sem,
              owner_of, strip, other, same, pair_far, pair_same, cols, live, near_out, near_in, ready,
              table_sem, load_sem, s1, r1, s2, r2, s3, r3, s4, r4, s5, r5, own_sem):
    depth, owners, ways, piece, sub, width, per_block, columns, share, early = geo
    subs = piece // sub
    chunks = [(k, i) for k in range(depth) for i in range(subs)]
    f = lax.axis_index("fsdp")
    r = lax.axis_index("replica")
    c, y = lax.rem(r, CORES), lax.div(r, CORES)
    mate = y * CORES + (1 - c)
    half = ways * piece

    def far_y(step):
        return lax.rem(y + step, ways)

    def far_f(step):
        if owners & (owners - 1):
            return lax.rem(f + step, owners)
        other_f, bit = f, 1
        while bit <= step:
            if step & bit:
                other_f = other_f + (1 - 2 * lax.rem(lax.div(f, bit), 2)) * bit
            bit *= 2
        return other_f

    barrier = pltpu.get_barrier_semaphore()
    pl.semaphore_signal(barrier, inc=1, device_id={"replica": mate}, device_id_type=MESH)
    for step in range(1, ways):
        pl.semaphore_signal(barrier, inc=1, device_id={"replica": far_y(step) * CORES + c}, device_id_type=MESH)
    for step in range(1, owners):
        pl.semaphore_signal(barrier, inc=1, device_id={"fsdp": far_f(step)}, device_id_type=MESH)
    names = pltpu.make_async_copy(table, owner_of, table_sem)
    names.start()
    pl.semaphore_wait(barrier, 1 + (ways - 1) + (owners - 1))

    pending = []

    def copy_to(src, dst, s, t, **to):
        return pltpu.make_async_remote_copy(
            src_ref=src, dst_ref=dst, send_sem=s, recv_sem=t, device_id=to, device_id_type=MESH
        )

    def send(src, dst, s, t, **to):
        copy = copy_to(src, dst, s, t, **to)
        copy.start()
        pending.append(copy)
        return copy

    pairs = {}

    def to_pair(step, i):
        into = other.at[step - 1, pl.ds(i * sub, sub)] if step else same.at[pl.ds(i * sub, sub)]
        start = pl.multiple_of((1 - c) * half + far_y(step) * piece + i * sub, 16)
        pairs[step, i] = send(grad.at[0, pl.ds(start, sub)], into, s1.at[step, i], r1.at[step, i], replica=mate)

    def near_rows(step):
        return pl.ds(pl.multiple_of(far_y(step) * piece, 16), piece)

    mine = {}
    for step in list(range(1, ways)) + [0]:
        for i in range(subs if step else 0):
            to_pair(step, i)
        start = pl.multiple_of(c * half + far_y(step) * piece, 16)
        mine[step] = pltpu.make_async_copy(grad.at[0, pl.ds(start, piece)], strip.at[near_rows(step)], load_sem.at[step])
        mine[step].start()
    names.wait()
    row = lax.div(f, per_block)

    names_here = [owner_of[row, col] for col in range(columns)]

    def place(d, carry):
        code = jnp.int32(0)
        for col in reversed(range(columns)):
            code = jnp.where(names_here[col] == d, code * (columns + 1) + (col + 1), code)
        for k in range(depth):
            digit = lax.rem(code, columns + 1)
            code = lax.div(code, columns + 1)
            cols[k, d] = jnp.maximum(digit - 1, 0)
            live[k, d] = jnp.minimum(digit, 1)
        return carry

    lax.fori_loop(0, owners, place, 0)

    def pair(step, i):
        pairs[step, i].wait_recv()
        low = pl.multiple_of(far_y(step) * piece + i * sub, 16)
        here = pl.ds(i * sub, sub)

        def add(col, carry):
            lanes = pl.ds(pl.multiple_of(col * width, 128), width)
            theirs = other[step - 1, here, lanes] if step else same[here, lanes]
            total = strip[pl.ds(low, sub), lanes].astype(jnp.float32) + theirs.astype(jnp.float32)
            if step:
                pair_far[step - 1, col, here, :] = total.astype(jnp.bfloat16)
            else:
                pair_same[col, here, :] = total
            return carry

        lax.fori_loop(0, columns, add, 0)

    second = {}

    def to_far(n):
        second[n] = []
        k, i = chunks[n]
        for step in range(1, ways):
            if k == 0:
                if i == 0:
                    mine[step].wait()
                pair(step, i)

            def pick(d, carry):
                near_out[n, step - 1, d] = pair_far[step - 1, cols[k, d], i * sub:(i + 1) * sub, :]
                return carry

            lax.fori_loop(0, owners, pick, 0)
            second[n].append(send(near_out.at[n, step - 1], near_in.at[n, step - 1], s2.at[n, step], r2.at[n, step],
                                  replica=far_y(step) * CORES + c))

    to_far(0)
    for i in range(subs):
        to_pair(0, i)
    if len(chunks) > 1:
        to_far(1)
    loads = [pltpu.make_async_copy(given[2].at[early], kept, early_in.at[0])]
    for i in range(4 if early else 0):
        loads.append(pltpu.make_async_copy(given[i].at[pl.ds(0, early)], held[i], early_in.at[i + 1]))
    for load in loads:
        load.start()
    mine[0].wait()
    for i in range(subs):
        pair(0, i)

    block_rows = owners // per_block

    def rows(m, source):
        k, j = m // block_rows, m % block_rows
        spot = lax.rem(source, CORES) * ways + lax.div(source, CORES)
        return out.at[k, pl.ds(j * per_block, per_block), spot]

    def row_of(n, source):
        k, i = chunks[n]
        return out.at[k, source, c * ways + y, pl.ds(i * sub, sub)]

    def arrived(n, source):
        @pl.when(f != source)
        def wait():
            copy_to(ready.at[n, 0], row_of(n, source), s3.at[n, 0], r3.at[n, source], fsdp=far_f(1)).wait_recv()

    third = {}

    def to_owners(n):
        for copy in second[n]:
            copy.wait_recv()
        for step in reversed(range(owners)):
            d = far_f(step)
            k, i = chunks[n]
            total = pair_same[cols[k, d], i * sub:(i + 1) * sub, :]
            for other_y in range(1, ways):
                total = total + near_in[n, other_y - 1, d].astype(jnp.float32)
            total = total * live[chunks[n][0], d].astype(jnp.float32)
            ready[n, step] = total.astype(jnp.bfloat16)
            if step == 0:
                third[n] = pltpu.make_async_copy(ready.at[n, 0], row_of(n, f), own_sem.at[n])
                third[n].start()
            else:
                send(ready.at[n, step], row_of(n, f), s3.at[n, step], r3.at[n, f], fsdp=d)

    fourth = {}

    def to_near(k):
        for n in range(k * subs, (k + 1) * subs):
            third[n].wait()
        for m in range(k * block_rows, (k + 1) * block_rows):
            fourth[m] = []
            for n in range(k * subs, (k + 1) * subs):
                for q in range(per_block):
                    arrived(n, (m % block_rows) * per_block + q)
            for step in range(1, ways):
                fourth[m].append(send(rows(m, r), rows(m, r), s4.at[m, step], r4.at[m, step],
                                      replica=far_y(step) * CORES + c))
            fourth[m].append(send(rows(m, r), rows(m, r), s5.at[m, 0], r5.at[m, 0], replica=mate))

    last = {}

    def to_mate(n):
        last[n] = [fourth[n][-1]]
        for step in range(1, ways):
            fourth[n][step - 1].wait_recv()
            source = lax.rem(y + ways - step, ways) * CORES + c
            last[n].append(send(rows(n, source), rows(n, source), s5.at[n, step], r5.at[n, step], replica=mate))

    def multiply(m):
        k, j = m // block_rows, m % block_rows
        for copy in last.pop(m):
            copy.wait_recv()
        left, right, lroot, rroot, update, block = held
        fetch = pltpu.make_async_copy(out.at[k, pl.ds(j * per_block, per_block)], block.at[m], block_sem.at[m])
        fetch.start()
        if m == 0:
            for load in loads[1:]:
                load.wait()
        fetch.wait()
        whole = block[m].reshape(width, width)
        columns_mine = block[m, :, :, :, lanes_of(share, r)].reshape(width, -1)
        strip_rows = ways * CORES * piece
        if share % strip_rows == 0:
            held_rows = block[m, pl.ds(r * (share // strip_rows), share // strip_rows)]
        else:
            first_piece = lax.div(lax.rem(r * share, strip_rows), piece)
            held_rows = block[m, lax.div(r * share, strip_rows), pl.ds(first_piece, share // piece)]
        value = products(share, r, whole, held_rows.reshape(share, width), columns_mine,
                         left.at[m], right.at[m], lroot.at[m], rroot.at[m])
        left[m], right[m], update[m] = value
        for i, source in enumerate((left, right, update)):
            stores.append(pltpu.make_async_copy(source.at[m], done[i].at[m], early_out.at[m, i]))
            stores[-1].start()

    stores = []
    count = len(chunks)
    for n in range(count):
        to_owners(n)
        if n + 2 < count:
            to_far(n + 2)
        if n >= subs and n % subs == 0:
            to_near(n // subs - 1)
    to_near(depth - 1)
    for m in range(early + 1):
        to_mate(m)
        if m < early:
            multiply(m)
    for copies in last.values():
        for copy in copies:
            copy.wait_recv()
    for copy in pending:
        copy.wait_send()
    loads[0].wait()
    for store in stores:
        store.wait()


def precondition(early, share, *refs):
    refs = list(refs)
    blocks, left, right, lroot, rroot = (refs.pop(0) for _ in range(5))
    ready = [refs.pop(0) for _ in range(3)] if early else []
    outs = [refs.pop(0) for _ in range(3)]
    block, mine, answer = refs.pop(0), [refs.pop(0) for _ in range(4)], refs.pop(0)
    in_sem, ready_sem, out_sem = refs
    r = lax.axis_index("replica")
    sources = [blocks.at[early], left.at[early], right.at[early], lroot, rroot.at[early]]
    fetches = [pltpu.make_async_copy(source, target, in_sem.at[i])
               for i, (source, target) in enumerate(zip(sources, [block] + mine))]
    for fetch in fetches:
        fetch.start()
    stores = []
    for i, source in enumerate(ready):
        stores.append(pltpu.make_async_copy(source, outs[i].at[pl.ds(0, early)], ready_sem.at[i]))
        stores[-1].start()
    for fetch in fetches:
        fetch.wait()
    rows = block[pl.ds(pl.multiple_of(r * share, 16), share), :]
    values = products(share, r, block[...], rows, block[:, lanes_of(share, r)], *mine)
    for i, target in enumerate((mine[0], mine[1], answer)):
        target[...] = values[i]
        stores.append(pltpu.make_async_copy(target, outs[i].at[early], out_sem.at[i]))
        stores[-1].start()
    for store in stores:
        store.wait()


def shards(gradients, left_factor, right_factor, left_root, right_root, owner_table):
    owners = lax.axis_size("fsdp")
    replicas = lax.axis_size("replica")
    ways = replicas // CORES
    strip_rows, total_cols = gradients.shape[1:]
    width = left_factor.shape[-1]
    depth, block_rows, share = left_factor.shape[1:4]
    columns = total_cols // width
    per_block = width // strip_rows
    piece = strip_rows // replicas
    sub = SUB if piece % SUB == 0 else piece
    chunks = depth * (piece // sub)
    hops = max(ways - 1, 1)
    total = depth * block_rows
    early = total - 1
    geo = (depth, owners, ways, piece, sub, width, per_block, columns, share, early)
    bf16 = jnp.bfloat16
    dma = pltpu.SemaphoreType.DMA
    vmem = [pltpu.VMEM(shape, kind) for shape, kind in (
        ((ways * piece, total_cols), bf16),
        ((hops, piece, total_cols), bf16),
        ((piece, total_cols), bf16),
        ((hops, columns, piece, width), bf16),
        ((columns, piece, width), jnp.float32),
        ((chunks, hops, owners, sub, width), bf16),
        ((chunks, hops, owners, sub, width), bf16),
        ((chunks, owners, sub, width), bf16),
    )]
    f32 = jnp.float32

    def parts(count):
        return [(count, share, width)] * 3 + [(count, width, width)]

    held = []
    if early:
        shapes = parts(early)
        held = [pltpu.VMEM(shape, kind) for shape, kind in zip(shapes, (f32, f32, bf16, bf16))]
        held += [pltpu.VMEM(shapes[0], bf16), pltpu.VMEM((early, per_block, replicas, piece, width), bf16)]
    planned = sum(math.prod(ref.shape) * jnp.dtype(ref.dtype).itemsize for ref in vmem + held) + 6 * 1024 * 1024
    given = [x.reshape(shape) for x, shape in
             zip((left_factor, right_factor, left_root, right_root), parts(total))]
    result = parts(total)[0]
    anywhere = pl.BlockSpec(memory_space=pl.ANY)
    first = [jax.ShapeDtypeStruct((depth, owners, replicas, piece, width), bf16),
             jax.ShapeDtypeStruct(result[1:], bf16)]
    if early:
        first += [jax.ShapeDtypeStruct((early,) + result[1:], kind) for kind in (f32, f32, bf16)]
    blocks, lroot, *ready = pl.pallas_call(
        functools.partial(exchange, geo),
        out_shape=tuple(first),
        in_specs=[pl.BlockSpec(memory_space=pltpu.HBM)] * 6,
        out_specs=(anywhere,) * len(first),
        scratch_shapes=held + [
            dma((5,)), dma((total, 3)), dma((total,)),
            pltpu.SMEM(owner_table.shape, jnp.int32),
            *vmem[:5],
            pltpu.SMEM((depth, owners), jnp.int32),
            pltpu.SMEM((depth, owners), jnp.int32),
            *vmem[5:],
            dma, dma((ways,)),
            dma((ways, piece // sub)), dma((ways, piece // sub)),
            dma((chunks, ways)), dma((chunks, ways)),
            dma((chunks, owners)), dma((chunks, owners)),
            dma((total, ways)), dma((total, ways)),
            dma((total, ways)), dma((total, ways)),
            dma((chunks,)),
        ],
        compiler_params=pltpu.CompilerParams(collective_id=0, has_side_effects=True, vmem_limit_bytes=planned),
    )(*(pltpu.with_memory_space_constraint(x, pltpu.HBM) for x in [owner_table, gradients] + given))
    blocks = blocks.reshape(total, width, width)

    shapes = parts(1)
    outs = (jax.ShapeDtypeStruct(result, f32), jax.ShapeDtypeStruct(result, f32), jax.ShapeDtypeStruct(result, bf16))
    results = pl.pallas_call(
        functools.partial(precondition, early, share),
        out_shape=outs,
        in_specs=[anywhere] * (5 + len(ready)),
        out_specs=(anywhere,) * 3,
        scratch_shapes=[
            pltpu.VMEM((width, width), bf16),
            pltpu.VMEM(shapes[0][1:], f32),
            pltpu.VMEM(shapes[0][1:], f32),
            pltpu.VMEM(shapes[0][1:], bf16),
            pltpu.VMEM(shapes[3][1:], bf16),
            pltpu.VMEM(shapes[0][1:], bf16),
            dma((5,)), dma((3,)), dma((3,)),
        ],
        compiler_params=pltpu.CompilerParams(vmem_limit_bytes=20 * 1024 * 1024),
    )(blocks, given[0], given[1], lroot, given[3], *ready)
    return tuple(x.reshape(left_factor.shape) for x in results)


def solution(mesh):
    placed = (
        P("replica", "fsdp", None),
        P("fsdp", None, None, "replica", None),
        P("fsdp", None, None, "replica", None),
        P("fsdp", None, None, "replica", None),
        P("fsdp", None, None, None, None),
        P(),
    )
    factors = P("fsdp", None, None, "replica", None)
    return jax.shard_map(
        shards,
        mesh=mesh,
        in_specs=placed,
        out_specs=(factors, factors, factors),
        check_vma=False,
    )
```

```python
import functools
import math

import jax
import jax.numpy as jnp
from jax import lax
from jax.experimental import pallas as pl
from jax.experimental.pallas import tpu as pltpu
from jax.sharding import PartitionSpec as P

decay_rate = 0.9
MESH = pl.DeviceIdType.MESH
CORES = 2
SUB = 16


def lanes_of(share, r):
    lanes = max(share, 128)
    return pl.ds(pl.multiple_of(lax.div(r, lanes // share) * lanes, 128), lanes)


def products(share, r, whole, rows, columns, left, right, lroot, rroot):
    scale = (1.0 - decay_rate) / whole.shape[0]
    shares = columns.shape[1] // share
    f32 = jnp.float32
    stat_left = lax.dot_general(rows, whole, (((1,), (1,)), ((), ())), preferred_element_type=f32)
    left_new = decay_rate * left[...] + scale * stat_left
    stat_right = lax.dot_general(columns, whole, (((0,), (0,)), ((), ())), preferred_element_type=f32)
    mine = stat_right[:share]
    for i in range(1, shares):
        mine = jnp.where(lax.rem(r, shares) == i, stat_right[i * share:(i + 1) * share], mine)
    right_new = decay_rate * right[...] + scale * mine
    half = jnp.dot(lroot[...], whole, preferred_element_type=f32).astype(jnp.bfloat16)
    update = jnp.dot(half, rroot[...], preferred_element_type=f32).astype(jnp.bfloat16)
    return left_new, right_new, update


def exchange(geo, table, grad, *refs):
    refs = list(refs)
    given = [refs.pop(0) for _ in range(4)]
    out, kept = refs.pop(0), refs.pop(0)
    done = [refs.pop(0) for _ in range(3)] if geo[-1] else []
    held = [refs.pop(0) for _ in range(6)] if geo[-1] else []
    early_in, early_out, block_sem = (refs.pop(0) for _ in range(3))
    _exchange(geo, table, grad, given, out, kept, done, held, early_in, early_out, block_sem, *refs)


def _exchange(geo, table, grad, given, out, kept, done, held, early_in, early_out, block_sem,
              owner_of, strip, other, same, pair_far, pair_same, cols, live, near_out, near_in, ready,
              table_sem, load_sem, s1, r1, s2, r2, s3, r3, s4, r4, s5, r5, own_sem):
    depth, owners, ways, piece, sub, width, per_block, columns, share, early = geo
    subs = piece // sub
    chunks = [(k, i) for k in range(depth) for i in range(subs)]
    f = lax.axis_index("fsdp")
    r = lax.axis_index("replica")
    c, y = lax.rem(r, CORES), lax.div(r, CORES)
    mate = y * CORES + (1 - c)
    half = ways * piece

    def far_y(step):
        return lax.rem(y + step, ways)

    def far_f(step):
        if owners & (owners - 1):
            return lax.rem(f + step, owners)
        other_f, bit = f, 1
        while bit <= step:
            if step & bit:
                other_f = other_f + (1 - 2 * lax.rem(lax.div(f, bit), 2)) * bit
            bit *= 2
        return other_f

    barrier = pltpu.get_barrier_semaphore()
    pl.semaphore_signal(barrier, inc=1, device_id={"replica": mate}, device_id_type=MESH)
    for step in range(1, ways):
        pl.semaphore_signal(barrier, inc=1, device_id={"replica": far_y(step) * CORES + c}, device_id_type=MESH)
    for step in range(1, owners):
        pl.semaphore_signal(barrier, inc=1, device_id={"fsdp": far_f(step)}, device_id_type=MESH)
    names = pltpu.make_async_copy(table, owner_of, table_sem)
    names.start()
    pl.semaphore_wait(barrier, 1 + (ways - 1) + (owners - 1))

    pending = []

    def copy_to(src, dst, s, t, **to):
        return pltpu.make_async_remote_copy(
            src_ref=src, dst_ref=dst, send_sem=s, recv_sem=t, device_id=to, device_id_type=MESH
        )

    def send(src, dst, s, t, **to):
        copy = copy_to(src, dst, s, t, **to)
        copy.start()
        pending.append(copy)
        return copy

    pairs = {}

    def to_pair(step, i):
        into = other.at[step - 1, pl.ds(i * sub, sub)] if step else same.at[pl.ds(i * sub, sub)]
        start = pl.multiple_of((1 - c) * half + far_y(step) * piece + i * sub, 16)
        pairs[step, i] = send(grad.at[0, pl.ds(start, sub)], into, s1.at[step, i], r1.at[step, i], replica=mate)

    def near_rows(step):
        return pl.ds(pl.multiple_of(far_y(step) * piece, 16), piece)

    mine = {}
    for step in list(range(1, ways)) + [0]:
        for i in range(subs if step else 0):
            to_pair(step, i)
        start = pl.multiple_of(c * half + far_y(step) * piece, 16)
        mine[step] = pltpu.make_async_copy(grad.at[0, pl.ds(start, piece)], strip.at[near_rows(step)], load_sem.at[step])
        mine[step].start()
    names.wait()
    row = lax.div(f, per_block)

    names_here = [owner_of[row, col] for col in range(columns)]

    def place(d, carry):
        code = jnp.int32(0)
        for col in reversed(range(columns)):
            code = jnp.where(names_here[col] == d, code * (columns + 1) + (col + 1), code)
        for k in range(depth):
            digit = lax.rem(code, columns + 1)
            code = lax.div(code, columns + 1)
            cols[k, d] = jnp.maximum(digit - 1, 0)
            live[k, d] = jnp.minimum(digit, 1)
        return carry

    lax.fori_loop(0, owners, place, 0)

    def pair(step, i):
        pairs[step, i].wait_recv()
        low = pl.multiple_of(far_y(step) * piece + i * sub, 16)
        here = pl.ds(i * sub, sub)

        def add(col, carry):
            lanes = pl.ds(pl.multiple_of(col * width, 128), width)
            theirs = other[step - 1, here, lanes] if step else same[here, lanes]
            total = strip[pl.ds(low, sub), lanes].astype(jnp.float32) + theirs.astype(jnp.float32)
            if step:
                pair_far[step - 1, col, here, :] = total.astype(jnp.bfloat16)
            else:
                pair_same[col, here, :] = total
            return carry

        lax.fori_loop(0, columns, add, 0)

    second = {}

    def to_far(n):
        second[n] = []
        k, i = chunks[n]
        for step in range(1, ways):
            if k == 0:
                if i == 0:
                    mine[step].wait()
                pair(step, i)

            def pick(d, carry):
                near_out[n, step - 1, d] = pair_far[step - 1, cols[k, d], i * sub:(i + 1) * sub, :]
                return carry

            lax.fori_loop(0, owners, pick, 0)
            second[n].append(send(near_out.at[n, step - 1], near_in.at[n, step - 1], s2.at[n, step], r2.at[n, step],
                                  replica=far_y(step) * CORES + c))

    to_far(0)
    for i in range(subs):
        to_pair(0, i)
    if len(chunks) > 1:
        to_far(1)
    loads = [pltpu.make_async_copy(given[2].at[early], kept, early_in.at[0])]
    for i in range(4 if early else 0):
        loads.append(pltpu.make_async_copy(given[i].at[pl.ds(0, early)], held[i], early_in.at[i + 1]))
    for load in loads:
        load.start()
    mine[0].wait()
    for i in range(subs):
        pair(0, i)

    block_rows = owners // per_block

    def rows(n, j, source):
        k, i = chunks[n]
        spot = lax.rem(source, CORES) * ways + lax.div(source, CORES)
        return out.at[k, pl.ds(j * per_block, per_block), spot, pl.ds(i * sub, sub)]

    def row_of(n, source):
        k, i = chunks[n]
        return out.at[k, source, c * ways + y, pl.ds(i * sub, sub)]

    def arrived(n, source):
        @pl.when(f != source)
        def wait():
            copy_to(ready.at[n, 0], row_of(n, source), s3.at[n, 0], r3.at[n, source], fsdp=far_f(1)).wait_recv()

    third = {}

    def to_owners(n):
        for copy in second[n]:
            copy.wait_recv()
        for step in reversed(range(owners)):
            d = far_f(step)
            k, i = chunks[n]
            total = pair_same[cols[k, d], i * sub:(i + 1) * sub, :]
            for other_y in range(1, ways):
                total = total + near_in[n, other_y - 1, d].astype(jnp.float32)
            total = total * live[chunks[n][0], d].astype(jnp.float32)
            ready[n, step] = total.astype(jnp.bfloat16)
            if step == 0:
                third[n] = pltpu.make_async_copy(ready.at[n, 0], row_of(n, f), own_sem.at[n])
                third[n].start()
            else:
                send(ready.at[n, step], row_of(n, f), s3.at[n, step], r3.at[n, f], fsdp=d)

    fourth = {}

    def to_near(n):
        third[n].wait()
        for j in range(block_rows):
            for q in range(per_block):
                arrived(n, j * per_block + q)
            u = n * block_rows + j
            here = rows(n, j, r)
            fourth[u] = []
            for step in range(1, ways):
                fourth[u].append(send(here, here, s4.at[u, step], r4.at[u, step], replica=far_y(step) * CORES + c))
            fourth[u].append(send(here, here, s5.at[u, 0], r5.at[u, 0], replica=mate))

    last = {}

    def to_mate(n, j):
        u = n * block_rows + j
        last[u] = [fourth[u][-1]]
        for step in range(1, ways):
            fourth[u][step - 1].wait_recv()
            there = rows(n, j, lax.rem(y + ways - step, ways) * CORES + c)
            last[u].append(send(there, there, s5.at[u, step], r5.at[u, step], replica=mate))

    def multiply(m):
        k, j = m // block_rows, m % block_rows
        for n in range(k * subs, (k + 1) * subs):
            for copy in last.pop(n * block_rows + j):
                copy.wait_recv()
        left, right, lroot, rroot, update, block = held
        fetch = pltpu.make_async_copy(out.at[k, pl.ds(j * per_block, per_block)], block.at[m], block_sem.at[m])
        fetch.start()
        if m == 0:
            for load in loads[1:]:
                load.wait()
        fetch.wait()
        whole = block[m].reshape(width, width)
        columns_mine = block[m, :, :, :, lanes_of(share, r)].reshape(width, -1)
        strip_rows = ways * CORES * piece
        if share % strip_rows == 0:
            held_rows = block[m, pl.ds(r * (share // strip_rows), share // strip_rows)]
        else:
            first_piece = lax.div(lax.rem(r * share, strip_rows), piece)
            held_rows = block[m, lax.div(r * share, strip_rows), pl.ds(first_piece, share // piece)]
        value = products(share, r, whole, held_rows.reshape(share, width), columns_mine,
                         left.at[m], right.at[m], lroot.at[m], rroot.at[m])
        left[m], right[m], update[m] = value
        for i, source in enumerate((left, right, update)):
            stores.append(pltpu.make_async_copy(source.at[m], done[i].at[m], early_out.at[m, i]))
            stores[-1].start()

    stores = []
    count = len(chunks)
    for n in range(count):
        to_owners(n)
        if n + 2 < count:
            to_far(n + 2)
        if n >= 2:
            to_near(n - 2)
    for n in range(count):
        if n == min(1, count - 1):
            for late in range(max(count - 2, 0), count):
                to_near(late)
        k = n // subs
        for j in range(block_rows):
            to_mate(n, j)
            if j and n % subs == subs - 1:
                multiply(k * block_rows + j - 1)
        if n % subs == subs - 1 and (k + 1) * block_rows <= early:
            multiply((k + 1) * block_rows - 1)
    for copies in last.values():
        for copy in copies:
            copy.wait_recv()
    for copy in pending:
        copy.wait_send()
    loads[0].wait()
    for store in stores:
        store.wait()


def precondition(early, share, *refs):
    refs = list(refs)
    blocks, left, right, lroot, rroot = (refs.pop(0) for _ in range(5))
    ready = [refs.pop(0) for _ in range(3)] if early else []
    outs = [refs.pop(0) for _ in range(3)]
    block, mine, answer = refs.pop(0), [refs.pop(0) for _ in range(4)], refs.pop(0)
    in_sem, ready_sem, out_sem = refs
    r = lax.axis_index("replica")
    sources = [blocks.at[early], left.at[early], right.at[early], lroot, rroot.at[early]]
    fetches = [pltpu.make_async_copy(source, target, in_sem.at[i])
               for i, (source, target) in enumerate(zip(sources, [block] + mine))]
    for fetch in fetches:
        fetch.start()
    stores = []
    for i, source in enumerate(ready):
        stores.append(pltpu.make_async_copy(source, outs[i].at[pl.ds(0, early)], ready_sem.at[i]))
        stores[-1].start()
    for fetch in fetches:
        fetch.wait()
    rows = block[pl.ds(pl.multiple_of(r * share, 16), share), :]
    values = products(share, r, block[...], rows, block[:, lanes_of(share, r)], *mine)
    for i, target in enumerate((mine[0], mine[1], answer)):
        target[...] = values[i]
        stores.append(pltpu.make_async_copy(target, outs[i].at[early], out_sem.at[i]))
        stores[-1].start()
    for store in stores:
        store.wait()


def shards(gradients, left_factor, right_factor, left_root, right_root, owner_table):
    owners = lax.axis_size("fsdp")
    replicas = lax.axis_size("replica")
    ways = replicas // CORES
    strip_rows, total_cols = gradients.shape[1:]
    width = left_factor.shape[-1]
    depth, block_rows, share = left_factor.shape[1:4]
    columns = total_cols // width
    per_block = width // strip_rows
    piece = strip_rows // replicas
    sub = SUB if piece % SUB == 0 else piece
    chunks = depth * (piece // sub)
    hops = max(ways - 1, 1)
    total = depth * block_rows
    early = total - 1
    geo = (depth, owners, ways, piece, sub, width, per_block, columns, share, early)
    bf16 = jnp.bfloat16
    dma = pltpu.SemaphoreType.DMA
    vmem = [pltpu.VMEM(shape, kind) for shape, kind in (
        ((ways * piece, total_cols), bf16),
        ((hops, piece, total_cols), bf16),
        ((piece, total_cols), bf16),
        ((hops, columns, piece, width), bf16),
        ((columns, piece, width), jnp.float32),
        ((chunks, hops, owners, sub, width), bf16),
        ((chunks, hops, owners, sub, width), bf16),
        ((chunks, owners, sub, width), bf16),
    )]
    f32 = jnp.float32

    def parts(count):
        return [(count, share, width)] * 3 + [(count, width, width)]

    held = []
    if early:
        shapes = parts(early)
        held = [pltpu.VMEM(shape, kind) for shape, kind in zip(shapes, (f32, f32, bf16, bf16))]
        held += [pltpu.VMEM(shapes[0], bf16), pltpu.VMEM((early, per_block, replicas, piece, width), bf16)]
    planned = sum(math.prod(ref.shape) * jnp.dtype(ref.dtype).itemsize for ref in vmem + held) + 6 * 1024 * 1024
    given = [x.reshape(shape) for x, shape in
             zip((left_factor, right_factor, left_root, right_root), parts(total))]
    result = parts(total)[0]
    anywhere = pl.BlockSpec(memory_space=pl.ANY)
    first = [jax.ShapeDtypeStruct((depth, owners, replicas, piece, width), bf16),
             jax.ShapeDtypeStruct(result[1:], bf16)]
    if early:
        first += [jax.ShapeDtypeStruct((early,) + result[1:], kind) for kind in (f32, f32, bf16)]
    blocks, lroot, *ready = pl.pallas_call(
        functools.partial(exchange, geo),
        out_shape=tuple(first),
        in_specs=[pl.BlockSpec(memory_space=pltpu.HBM)] * 6,
        out_specs=(anywhere,) * len(first),
        scratch_shapes=held + [
            dma((5,)), dma((total, 3)), dma((total,)),
            pltpu.SMEM(owner_table.shape, jnp.int32),
            *vmem[:5],
            pltpu.SMEM((depth, owners), jnp.int32),
            pltpu.SMEM((depth, owners), jnp.int32),
            *vmem[5:],
            dma, dma((ways,)),
            dma((ways, piece // sub)), dma((ways, piece // sub)),
            dma((chunks, ways)), dma((chunks, ways)),
            dma((chunks, owners)), dma((chunks, owners)),
            dma((chunks * block_rows, ways)), dma((chunks * block_rows, ways)),
            dma((chunks * block_rows, ways)), dma((chunks * block_rows, ways)),
            dma((chunks,)),
        ],
        compiler_params=pltpu.CompilerParams(collective_id=0, has_side_effects=True, vmem_limit_bytes=planned),
    )(*(pltpu.with_memory_space_constraint(x, pltpu.HBM) for x in [owner_table, gradients] + given))
    blocks = blocks.reshape(total, width, width)

    shapes = parts(1)
    outs = (jax.ShapeDtypeStruct(result, f32), jax.ShapeDtypeStruct(result, f32), jax.ShapeDtypeStruct(result, bf16))
    results = pl.pallas_call(
        functools.partial(precondition, early, share),
        out_shape=outs,
        in_specs=[anywhere] * (5 + len(ready)),
        out_specs=(anywhere,) * 3,
        scratch_shapes=[
            pltpu.VMEM((width, width), bf16),
            pltpu.VMEM(shapes[0][1:], f32),
            pltpu.VMEM(shapes[0][1:], f32),
            pltpu.VMEM(shapes[0][1:], bf16),
            pltpu.VMEM(shapes[3][1:], bf16),
            pltpu.VMEM(shapes[0][1:], bf16),
            dma((5,)), dma((3,)), dma((3,)),
        ],
        compiler_params=pltpu.CompilerParams(vmem_limit_bytes=20 * 1024 * 1024),
    )(blocks, given[0], given[1], lroot, given[3], *ready)
    return tuple(x.reshape(left_factor.shape) for x in results)


def solution(mesh):
    placed = (
        P("replica", "fsdp", None),
        P("fsdp", None, None, "replica", None),
        P("fsdp", None, None, "replica", None),
        P("fsdp", None, None, "replica", None),
        P("fsdp", None, None, None, None),
        P(),
    )
    factors = P("fsdp", None, None, "replica", None)
    return jax.shard_map(
        shards,
        mesh=mesh,
        in_specs=placed,
        out_specs=(factors, factors, factors),
        check_vma=False,
    )
```

```python
import functools
import math

import jax
import jax.numpy as jnp
from jax import lax
from jax.experimental import pallas as pl
from jax.experimental.pallas import tpu as pltpu
from jax.sharding import PartitionSpec as P

decay_rate = 0.9
MESH = pl.DeviceIdType.MESH
CORES = 2
SUB = 16


def lanes_of(share, r):
    lanes = max(share, 128)
    return pl.ds(pl.multiple_of(lax.div(r, lanes // share) * lanes, 128), lanes)


def products(share, r, whole, rows, columns, left, right, lroot, rroot):
    scale = (1.0 - decay_rate) / whole.shape[0]
    shares = columns.shape[1] // share
    f32 = jnp.float32
    stat_left = lax.dot_general(rows, whole, (((1,), (1,)), ((), ())), preferred_element_type=f32)
    left_new = decay_rate * left[...] + scale * stat_left
    stat_right = lax.dot_general(columns, whole, (((0,), (0,)), ((), ())), preferred_element_type=f32)
    mine = stat_right[:share]
    for i in range(1, shares):
        mine = jnp.where(lax.rem(r, shares) == i, stat_right[i * share:(i + 1) * share], mine)
    right_new = decay_rate * right[...] + scale * mine
    half = jnp.dot(lroot[...], whole, preferred_element_type=f32).astype(jnp.bfloat16)
    update = jnp.dot(half, rroot[...], preferred_element_type=f32).astype(jnp.bfloat16)
    return left_new, right_new, update


def exchange(geo, table, grad, *refs):
    refs = list(refs)
    given = [refs.pop(0) for _ in range(4)]
    out, kept = refs.pop(0), refs.pop(0)
    done = [refs.pop(0) for _ in range(3)] if geo[-1] else []
    held = [refs.pop(0) for _ in range(6)] if geo[-1] else []
    early_in, early_out, block_sem = (refs.pop(0) for _ in range(3))
    _exchange(geo, table, grad, given, out, kept, done, held, early_in, early_out, block_sem, *refs)


def _exchange(geo, table, grad, given, out, kept, done, held, early_in, early_out, block_sem,
              owner_of, strip, other, same, pair_far, pair_same, cols, live, near_out, near_in, ready,
              here, table_sem, load_sem, s1, r1, s2, r2, s3, r3, s4, r4, s5, r5, own_sem):
    depth, owners, ways, piece, sub, width, per_block, columns, share, early = geo
    subs = piece // sub
    chunks = [(k, i) for k in range(depth) for i in range(subs)]
    f = lax.axis_index("fsdp")
    r = lax.axis_index("replica")
    c, y = lax.rem(r, CORES), lax.div(r, CORES)
    mate = y * CORES + (1 - c)
    half = ways * piece

    def far_y(step):
        return lax.rem(y + step, ways)

    def far_f(step):
        if owners & (owners - 1):
            return lax.rem(f + step, owners)
        other_f, bit = f, 1
        while bit <= step:
            if step & bit:
                other_f = other_f + (1 - 2 * lax.rem(lax.div(f, bit), 2)) * bit
            bit *= 2
        return other_f

    barrier = pltpu.get_barrier_semaphore()
    met_mate, met_y, met_y_mates, met_owners = (here.at[i] for i in range(4))

    def tell(sem, **to):
        pl.semaphore_signal(sem, inc=1, device_id=to, device_id_type=MESH)

    @pl.when(c == 1)
    def side_enters():
        tell(barrier, replica=mate)

    @pl.when(c == 0)
    def lead_enters():
        for step in range(1, ways):
            tell(barrier, replica=far_y(step) * CORES)
        pl.semaphore_wait(barrier, ways)
        tell(met_mate, replica=mate)
        for step in range(1, ways):
            tell(met_y, replica=far_y(step) * CORES)

    @pl.when(c == 1)
    def side_goes_on():
        pl.semaphore_wait(met_mate, 1)
        for step in range(1, owners):
            tell(barrier, fsdp=far_f(step))

    names = pltpu.make_async_copy(table, owner_of, table_sem)
    names.start()

    pending = []

    def copy_to(src, dst, s, t, **to):
        return pltpu.make_async_remote_copy(
            src_ref=src, dst_ref=dst, send_sem=s, recv_sem=t, device_id=to, device_id_type=MESH
        )

    def send(src, dst, s, t, **to):
        copy = copy_to(src, dst, s, t, **to)
        copy.start()
        pending.append(copy)
        return copy

    pairs = {}

    def to_pair(step, i):
        into = other.at[step - 1, pl.ds(i * sub, sub)] if step else same.at[pl.ds(i * sub, sub)]
        start = pl.multiple_of((1 - c) * half + far_y(step) * piece + i * sub, 16)
        pairs[step, i] = send(grad.at[0, pl.ds(start, sub)], into, s1.at[step, i], r1.at[step, i], replica=mate)

    def near_rows(step):
        return pl.ds(pl.multiple_of(far_y(step) * piece, 16), piece)

    mine = {}
    for step in list(range(1, ways)) + [0]:
        for i in range(subs if step else 0):
            to_pair(step, i)
        start = pl.multiple_of(c * half + far_y(step) * piece, 16)
        mine[step] = pltpu.make_async_copy(grad.at[0, pl.ds(start, piece)], strip.at[near_rows(step)], load_sem.at[step])
        mine[step].start()
    @pl.when(c == 0)
    def lead_knows_y():
        if ways > 1:
            pl.semaphore_wait(met_y, ways - 1)
        tell(met_y_mates, replica=mate)

    names.wait()
    row = lax.div(f, per_block)

    names_here = [owner_of[row, col] for col in range(columns)]

    def place(d, carry):
        code = jnp.int32(0)
        for col in reversed(range(columns)):
            code = jnp.where(names_here[col] == d, code * (columns + 1) + (col + 1), code)
        for k in range(depth):
            digit = lax.rem(code, columns + 1)
            code = lax.div(code, columns + 1)
            cols[k, d] = jnp.maximum(digit - 1, 0)
            live[k, d] = jnp.minimum(digit, 1)
        return carry

    lax.fori_loop(0, owners, place, 0)

    def pair(step, i):
        pairs[step, i].wait_recv()
        low = pl.multiple_of(far_y(step) * piece + i * sub, 16)
        here = pl.ds(i * sub, sub)

        def add(col, carry):
            lanes = pl.ds(pl.multiple_of(col * width, 128), width)
            theirs = other[step - 1, here, lanes] if step else same[here, lanes]
            total = strip[pl.ds(low, sub), lanes].astype(jnp.float32) + theirs.astype(jnp.float32)
            if step:
                pair_far[step - 1, col, here, :] = total.astype(jnp.bfloat16)
            else:
                pair_same[col, here, :] = total
            return carry

        lax.fori_loop(0, columns, add, 0)

    second = {}

    def to_far(n):
        second[n] = []
        k, i = chunks[n]
        for step in range(1, ways):
            if k == 0:
                if i == 0:
                    mine[step].wait()
                pair(step, i)

            def pick(d, carry):
                near_out[n, step - 1, d] = pair_far[step - 1, cols[k, d], i * sub:(i + 1) * sub, :]
                return carry

            lax.fori_loop(0, owners, pick, 0)
            second[n].append(send(near_out.at[n, step - 1], near_in.at[n, step - 1], s2.at[n, step], r2.at[n, step],
                                  replica=far_y(step) * CORES + c))

    @pl.when(c == 1)
    def side_knows_y():
        pl.semaphore_wait(met_y_mates, 1)

    to_far(0)
    for i in range(subs):
        to_pair(0, i)
    if len(chunks) > 1:
        to_far(1)
    loads = [pltpu.make_async_copy(given[2].at[early], kept, early_in.at[0])]
    for i in range(4 if early else 0):
        loads.append(pltpu.make_async_copy(given[i].at[pl.ds(0, early)], held[i], early_in.at[i + 1]))
    for load in loads:
        load.start()
    mine[0].wait()
    for i in range(subs):
        pair(0, i)

    @pl.when(c == 1)
    def side_knows_owners():
        pl.semaphore_wait(barrier, owners - 1)
        tell(met_owners, replica=mate)

    @pl.when(c == 0)
    def lead_knows_owners():
        pl.semaphore_wait(met_owners, 1)

    block_rows = owners // per_block

    def rows(n, j, source):
        k, i = chunks[n]
        spot = lax.rem(source, CORES) * ways + lax.div(source, CORES)
        return out.at[k, pl.ds(j * per_block, per_block), spot, pl.ds(i * sub, sub)]

    def row_of(n, source):
        k, i = chunks[n]
        return out.at[k, source, c * ways + y, pl.ds(i * sub, sub)]

    def arrived(n, source):
        @pl.when(f != source)
        def wait():
            copy_to(ready.at[n, 0], row_of(n, source), s3.at[n, 0], r3.at[n, source], fsdp=far_f(1)).wait_recv()

    third = {}

    def to_owners(n):
        for copy in second[n]:
            copy.wait_recv()
        for step in reversed(range(owners)):
            d = far_f(step)
            k, i = chunks[n]
            total = pair_same[cols[k, d], i * sub:(i + 1) * sub, :]
            for other_y in range(1, ways):
                total = total + near_in[n, other_y - 1, d].astype(jnp.float32)
            total = total * live[chunks[n][0], d].astype(jnp.float32)
            ready[n, step] = total.astype(jnp.bfloat16)
            if step == 0:
                third[n] = pltpu.make_async_copy(ready.at[n, 0], row_of(n, f), own_sem.at[n])
                third[n].start()
            else:
                send(ready.at[n, step], row_of(n, f), s3.at[n, step], r3.at[n, f], fsdp=d)

    fourth = {}

    def to_near(n):
        third[n].wait()
        for j in range(block_rows):
            for q in range(per_block):
                arrived(n, j * per_block + q)
            u = n * block_rows + j
            mine_now = rows(n, j, r)
            fourth[u] = []
            for step in range(1, ways):
                fourth[u].append(send(mine_now, mine_now, s4.at[u, step], r4.at[u, step], replica=far_y(step) * CORES + c))
            fourth[u].append(send(mine_now, mine_now, s5.at[u, 0], r5.at[u, 0], replica=mate))

    last = {}

    def to_mate(n, j):
        u = n * block_rows + j
        last[u] = [fourth[u][-1]]
        for step in range(1, ways):
            fourth[u][step - 1].wait_recv()
            there = rows(n, j, lax.rem(y + ways - step, ways) * CORES + c)
            last[u].append(send(there, there, s5.at[u, step], r5.at[u, step], replica=mate))

    def multiply(m):
        k, j = m // block_rows, m % block_rows
        for n in range(k * subs, (k + 1) * subs):
            for copy in last.pop(n * block_rows + j):
                copy.wait_recv()
        left, right, lroot, rroot, update, block = held
        fetch = pltpu.make_async_copy(out.at[k, pl.ds(j * per_block, per_block)], block.at[m], block_sem.at[m])
        fetch.start()
        if m == 0:
            for load in loads[1:]:
                load.wait()
        fetch.wait()
        whole = block[m].reshape(width, width)
        columns_mine = block[m, :, :, :, lanes_of(share, r)].reshape(width, -1)
        strip_rows = ways * CORES * piece
        if share % strip_rows == 0:
            held_rows = block[m, pl.ds(r * (share // strip_rows), share // strip_rows)]
        else:
            first_piece = lax.div(lax.rem(r * share, strip_rows), piece)
            held_rows = block[m, lax.div(r * share, strip_rows), pl.ds(first_piece, share // piece)]
        value = products(share, r, whole, held_rows.reshape(share, width), columns_mine,
                         left.at[m], right.at[m], lroot.at[m], rroot.at[m])
        left[m], right[m], update[m] = value
        for i, source in enumerate((left, right, update)):
            stores.append(pltpu.make_async_copy(source.at[m], done[i].at[m], early_out.at[m, i]))
            stores[-1].start()

    stores = []
    count = len(chunks)
    for n in range(count):
        to_owners(n)
        if n + 2 < count:
            to_far(n + 2)
        if n >= 2:
            to_near(n - 2)
    for n in range(count):
        if n == min(1, count - 1):
            for late in range(max(count - 2, 0), count):
                to_near(late)
        k = n // subs
        for j in range(block_rows):
            to_mate(n, j)
            if j and n % subs == subs - 1:
                multiply(k * block_rows + j - 1)
        if n % subs == subs - 1 and (k + 1) * block_rows <= early:
            multiply((k + 1) * block_rows - 1)
    for copies in last.values():
        for copy in copies:
            copy.wait_recv()
    for copy in pending:
        copy.wait_send()
    loads[0].wait()
    for store in stores:
        store.wait()


def precondition(early, share, *refs):
    refs = list(refs)
    blocks, left, right, lroot, rroot = (refs.pop(0) for _ in range(5))
    ready = [refs.pop(0) for _ in range(3)] if early else []
    outs = [refs.pop(0) for _ in range(3)]
    block, mine, answer = refs.pop(0), [refs.pop(0) for _ in range(4)], refs.pop(0)
    in_sem, ready_sem, out_sem = refs
    r = lax.axis_index("replica")
    sources = [blocks.at[early], left.at[early], right.at[early], lroot, rroot.at[early]]
    fetches = [pltpu.make_async_copy(source, target, in_sem.at[i])
               for i, (source, target) in enumerate(zip(sources, [block] + mine))]
    for fetch in fetches:
        fetch.start()
    stores = []
    for i, source in enumerate(ready):
        stores.append(pltpu.make_async_copy(source, outs[i].at[pl.ds(0, early)], ready_sem.at[i]))
        stores[-1].start()
    for fetch in fetches:
        fetch.wait()
    rows = block[pl.ds(pl.multiple_of(r * share, 16), share), :]
    values = products(share, r, block[...], rows, block[:, lanes_of(share, r)], *mine)
    for i, target in enumerate((mine[0], mine[1], answer)):
        target[...] = values[i]
        stores.append(pltpu.make_async_copy(target, outs[i].at[early], out_sem.at[i]))
        stores[-1].start()
    for store in stores:
        store.wait()


def shards(gradients, left_factor, right_factor, left_root, right_root, owner_table):
    owners = lax.axis_size("fsdp")
    replicas = lax.axis_size("replica")
    ways = replicas // CORES
    strip_rows, total_cols = gradients.shape[1:]
    width = left_factor.shape[-1]
    depth, block_rows, share = left_factor.shape[1:4]
    columns = total_cols // width
    per_block = width // strip_rows
    piece = strip_rows // replicas
    sub = SUB if piece % SUB == 0 else piece
    chunks = depth * (piece // sub)
    hops = max(ways - 1, 1)
    total = depth * block_rows
    early = total - 1
    geo = (depth, owners, ways, piece, sub, width, per_block, columns, share, early)
    bf16 = jnp.bfloat16
    dma = pltpu.SemaphoreType.DMA
    vmem = [pltpu.VMEM(shape, kind) for shape, kind in (
        ((ways * piece, total_cols), bf16),
        ((hops, piece, total_cols), bf16),
        ((piece, total_cols), bf16),
        ((hops, columns, piece, width), bf16),
        ((columns, piece, width), jnp.float32),
        ((chunks, hops, owners, sub, width), bf16),
        ((chunks, hops, owners, sub, width), bf16),
        ((chunks, owners, sub, width), bf16),
    )]
    f32 = jnp.float32

    def parts(count):
        return [(count, share, width)] * 3 + [(count, width, width)]

    held = []
    if early:
        shapes = parts(early)
        held = [pltpu.VMEM(shape, kind) for shape, kind in zip(shapes, (f32, f32, bf16, bf16))]
        held += [pltpu.VMEM(shapes[0], bf16), pltpu.VMEM((early, per_block, replicas, piece, width), bf16)]
    planned = sum(math.prod(ref.shape) * jnp.dtype(ref.dtype).itemsize for ref in vmem + held) + 6 * 1024 * 1024
    given = [x.reshape(shape) for x, shape in
             zip((left_factor, right_factor, left_root, right_root), parts(total))]
    result = parts(total)[0]
    anywhere = pl.BlockSpec(memory_space=pl.ANY)
    first = [jax.ShapeDtypeStruct((depth, owners, replicas, piece, width), bf16),
             jax.ShapeDtypeStruct(result[1:], bf16)]
    if early:
        first += [jax.ShapeDtypeStruct((early,) + result[1:], kind) for kind in (f32, f32, bf16)]
    blocks, lroot, *ready = pl.pallas_call(
        functools.partial(exchange, geo),
        out_shape=tuple(first),
        in_specs=[pl.BlockSpec(memory_space=pltpu.HBM)] * 6,
        out_specs=(anywhere,) * len(first),
        scratch_shapes=held + [
            dma((5,)), dma((total, 3)), dma((total,)),
            pltpu.SMEM(owner_table.shape, jnp.int32),
            *vmem[:5],
            pltpu.SMEM((depth, owners), jnp.int32),
            pltpu.SMEM((depth, owners), jnp.int32),
            *vmem[5:],
            pltpu.SemaphoreType.REGULAR((4,)),
            dma, dma((ways,)),
            dma((ways, piece // sub)), dma((ways, piece // sub)),
            dma((chunks, ways)), dma((chunks, ways)),
            dma((chunks, owners)), dma((chunks, owners)),
            dma((chunks * block_rows, ways)), dma((chunks * block_rows, ways)),
            dma((chunks * block_rows, ways)), dma((chunks * block_rows, ways)),
            dma((chunks,)),
        ],
        compiler_params=pltpu.CompilerParams(collective_id=0, has_side_effects=True, vmem_limit_bytes=planned),
    )(*(pltpu.with_memory_space_constraint(x, pltpu.HBM) for x in [owner_table, gradients] + given))
    blocks = blocks.reshape(total, width, width)

    shapes = parts(1)
    outs = (jax.ShapeDtypeStruct(result, f32), jax.ShapeDtypeStruct(result, f32), jax.ShapeDtypeStruct(result, bf16))
    results = pl.pallas_call(
        functools.partial(precondition, early, share),
        out_shape=outs,
        in_specs=[anywhere] * (5 + len(ready)),
        out_specs=(anywhere,) * 3,
        scratch_shapes=[
            pltpu.VMEM((width, width), bf16),
            pltpu.VMEM(shapes[0][1:], f32),
            pltpu.VMEM(shapes[0][1:], f32),
            pltpu.VMEM(shapes[0][1:], bf16),
            pltpu.VMEM(shapes[3][1:], bf16),
            pltpu.VMEM(shapes[0][1:], bf16),
            dma((5,)), dma((3,)), dma((3,)),
        ],
        compiler_params=pltpu.CompilerParams(vmem_limit_bytes=20 * 1024 * 1024),
    )(blocks, given[0], given[1], lroot, given[3], *ready)
    return tuple(x.reshape(left_factor.shape) for x in results)


def solution(mesh):
    placed = (
        P("replica", "fsdp", None),
        P("fsdp", None, None, "replica", None),
        P("fsdp", None, None, "replica", None),
        P("fsdp", None, None, "replica", None),
        P("fsdp", None, None, None, None),
        P(),
    )
    factors = P("fsdp", None, None, "replica", None)
    return jax.shard_map(
        shards,
        mesh=mesh,
        in_specs=placed,
        out_specs=(factors, factors, factors),
        check_vma=False,
    )
```

```python
import functools
import math

import jax
import jax.numpy as jnp
from jax import lax
from jax.experimental import pallas as pl
from jax.experimental.pallas import tpu as pltpu
from jax.sharding import PartitionSpec as P

decay_rate = 0.9
MESH = pl.DeviceIdType.MESH
CORES = 2
SUB = 16


def lanes_of(share, r):
    lanes = max(share, 128)
    return pl.ds(pl.multiple_of(lax.div(r, lanes // share) * lanes, 128), lanes)


def products(share, r, whole, rows, columns, left, right, lroot, rroot):
    scale = (1.0 - decay_rate) / whole.shape[0]
    shares = columns.shape[1] // share
    f32 = jnp.float32
    stat_left = lax.dot_general(rows, whole, (((1,), (1,)), ((), ())), preferred_element_type=f32)
    left_new = decay_rate * left[...] + scale * stat_left
    stat_right = lax.dot_general(columns, whole, (((0,), (0,)), ((), ())), preferred_element_type=f32)
    mine = stat_right[:share]
    for i in range(1, shares):
        mine = jnp.where(lax.rem(r, shares) == i, stat_right[i * share:(i + 1) * share], mine)
    right_new = decay_rate * right[...] + scale * mine
    half = jnp.dot(lroot[...], whole, preferred_element_type=f32).astype(jnp.bfloat16)
    update = jnp.dot(half, rroot[...], preferred_element_type=f32).astype(jnp.bfloat16)
    return left_new, right_new, update


def exchange(geo, table, grad, *refs):
    refs = list(refs)
    given = [refs.pop(0) for _ in range(4)]
    out, kept = refs.pop(0), refs.pop(0)
    done = [refs.pop(0) for _ in range(3)] if geo[-1] else []
    held = [refs.pop(0) for _ in range(6)] if geo[-1] else []
    early_in, early_out, block_sem = (refs.pop(0) for _ in range(3))
    _exchange(geo, table, grad, given, out, kept, done, held, early_in, early_out, block_sem, *refs)


def _exchange(geo, table, grad, given, out, kept, done, held, early_in, early_out, block_sem,
              owner_of, strip, other, same, pair_far, pair_same, cols, live, near_out, near_in, ready,
              here, table_sem, load_sem, s1, r1, s2, r2, s3, r3, s4, r4, s5, r5, own_sem):
    depth, owners, ways, piece, sub, width, per_block, columns, share, early = geo
    subs = piece // sub
    chunks = [(k, i) for k in range(depth) for i in range(subs)]
    count = len(chunks)
    f = lax.axis_index("fsdp")
    r = lax.axis_index("replica")
    c, y = lax.rem(r, CORES), lax.div(r, CORES)
    mate = y * CORES + (1 - c)
    half = ways * piece

    def far_y(step):
        return lax.rem(y + step, ways)

    def far_f(step):
        if owners & (owners - 1):
            return lax.rem(f + step, owners)
        other_f, bit = f, 1
        while bit <= step:
            if step & bit:
                other_f = other_f + (1 - 2 * lax.rem(lax.div(f, bit), 2)) * bit
            bit *= 2
        return other_f

    barrier = pltpu.get_barrier_semaphore()
    met_mate, met_y, met_y_mates, met_owners = (here.at[i] for i in range(4))

    def tell(sem, **to):
        pl.semaphore_signal(sem, inc=1, device_id=to, device_id_type=MESH)

    @pl.when(c == 1)
    def side_enters():
        tell(barrier, replica=mate)

    @pl.when(c == 0)
    def lead_enters():
        for step in range(1, ways):
            tell(barrier, replica=far_y(step) * CORES)
        pl.semaphore_wait(barrier, ways)
        tell(met_mate, replica=mate)
        for step in range(1, ways):
            tell(met_y, replica=far_y(step) * CORES)

    @pl.when(c == 1)
    def side_goes_on():
        pl.semaphore_wait(met_mate, 1)
        for step in range(1, owners):
            tell(barrier, fsdp=far_f(step))

    names = pltpu.make_async_copy(table, owner_of, table_sem)
    names.start()

    pending = []

    def copy_to(src, dst, s, t, **to):
        return pltpu.make_async_remote_copy(
            src_ref=src, dst_ref=dst, send_sem=s, recv_sem=t, device_id=to, device_id_type=MESH
        )

    def send(src, dst, s, t, **to):
        copy = copy_to(src, dst, s, t, **to)
        copy.start()
        pending.append(copy)
        return copy

    pairs = {}

    def to_pair(step, i):
        into = other.at[step - 1, pl.ds(i * sub, sub)] if step else same.at[pl.ds(i * sub, sub)]
        start = pl.multiple_of((1 - c) * half + far_y(step) * piece + i * sub, 16)
        pairs[step, i] = send(grad.at[0, pl.ds(start, sub)], into, s1.at[step, i], r1.at[step, i], replica=mate)

    def near_rows(step):
        return pl.ds(pl.multiple_of(far_y(step) * piece, 16), piece)

    mine = {}
    for step in list(range(1, ways)) + [0]:
        for i in range(subs if step else 0):
            to_pair(step, i)
        start = pl.multiple_of(c * half + far_y(step) * piece, 16)
        mine[step] = pltpu.make_async_copy(grad.at[0, pl.ds(start, piece)], strip.at[near_rows(step)], load_sem.at[step])
        mine[step].start()
    @pl.when(c == 0)
    def lead_knows_y():
        if ways > 1:
            pl.semaphore_wait(met_y, ways - 1)
        tell(met_y_mates, replica=mate)

    names.wait()
    row = lax.div(f, per_block)

    names_here = [owner_of[row, col] for col in range(columns)]

    def place(d, carry):
        code = jnp.int32(0)
        for col in reversed(range(columns)):
            code = jnp.where(names_here[col] == d, code * (columns + 1) + (col + 1), code)
        for k in range(depth):
            digit = lax.rem(code, columns + 1)
            code = lax.div(code, columns + 1)
            cols[k, d] = jnp.maximum(digit - 1, 0)
            live[k, d] = jnp.minimum(digit, 1)
        return carry

    lax.fori_loop(0, owners, place, 0)

    def pair(step, i):
        pairs[step, i].wait_recv()
        low = pl.multiple_of(far_y(step) * piece + i * sub, 16)
        here = pl.ds(i * sub, sub)

        def add(col, carry):
            lanes = pl.ds(pl.multiple_of(col * width, 128), width)
            theirs = other[step - 1, here, lanes] if step else same[here, lanes]
            total = strip[pl.ds(low, sub), lanes].astype(jnp.float32) + theirs.astype(jnp.float32)
            if step:
                pair_far[step - 1, col, here, :] = total.astype(jnp.bfloat16)
            else:
                pair_same[col, here, :] = total
            return carry

        lax.fori_loop(0, columns, add, 0)

    second = {}

    def to_far(n):
        second[n] = []
        k, i = chunks[n]
        for step in range(1, ways):
            if k == 0:
                if i == 0:
                    mine[step].wait()
                pair(step, i)

            def pick(d, carry):
                near_out[n, step - 1, d] = pair_far[step - 1, cols[k, d], i * sub:(i + 1) * sub, :]
                return carry

            lax.fori_loop(0, owners, pick, 0)
            second[n].append(send(near_out.at[n, step - 1], near_in.at[n, step - 1], s2.at[n, step], r2.at[n, step],
                                  replica=far_y(step) * CORES + c))

    @pl.when(c == 1)
    def side_knows_y():
        pl.semaphore_wait(met_y_mates, 1)

    to_far(0)
    for i in range(subs):
        to_pair(0, i)
    if len(chunks) > 1:
        to_far(1)
    loads = [pltpu.make_async_copy(given[2].at[early], kept, early_in.at[0])]
    for i in range(4 if early else 0):
        loads.append(pltpu.make_async_copy(given[i].at[pl.ds(0, early)], held[i], early_in.at[i + 1]))
    for load in loads:
        load.start()
    mine[0].wait()
    for i in range(subs):
        pair(0, i)

    @pl.when(c == 1)
    def side_knows_owners():
        pl.semaphore_wait(barrier, owners - 1)
        tell(met_owners, replica=mate)

    @pl.when(c == 0)
    def lead_knows_owners():
        pl.semaphore_wait(met_owners, 1)

    block_rows = owners // per_block

    def rows(n, j, source):
        k, i = chunks[n]
        spot = lax.rem(source, CORES) * ways + lax.div(source, CORES)
        return out.at[k, pl.ds(j * per_block, per_block), spot, pl.ds(i * sub, sub)]

    def row_of(n, source):
        k, i = chunks[n]
        return out.at[k, source, c * ways + y, pl.ds(i * sub, sub)]

    def arrived(n, source):
        @pl.when(f != source)
        def wait():
            copy_to(ready.at[n, 0], row_of(n, source), s3.at[n, 0], r3.at[n, source], fsdp=far_f(1)).wait_recv()

    third = {}

    def to_owners(n):
        for copy in second[n]:
            copy.wait_recv()
        if n >= 2 and n == count - 1:
            for early_chunk in range(n - 1):
                to_near(early_chunk)
        for step in reversed(range(owners)):
            d = far_f(step)
            k, i = chunks[n]
            total = pair_same[cols[k, d], i * sub:(i + 1) * sub, :]
            for other_y in range(1, ways):
                total = total + near_in[n, other_y - 1, d].astype(jnp.float32)
            total = total * live[chunks[n][0], d].astype(jnp.float32)
            ready[n, step] = total.astype(jnp.bfloat16)
            if step == 0:
                third[n] = pltpu.make_async_copy(ready.at[n, 0], row_of(n, f), own_sem.at[n])
                third[n].start()
            else:
                send(ready.at[n, step], row_of(n, f), s3.at[n, step], r3.at[n, f], fsdp=d)

    fourth = {}

    def to_near(n):
        third[n].wait()
        for j in range(block_rows):
            for q in range(per_block):
                arrived(n, j * per_block + q)
            u = n * block_rows + j
            mine_now = rows(n, j, r)
            fourth[u] = []
            for step in range(1, ways):
                fourth[u].append(send(mine_now, mine_now, s4.at[u, step], r4.at[u, step], replica=far_y(step) * CORES + c))
            fourth[u].append(send(mine_now, mine_now, s5.at[u, 0], r5.at[u, 0], replica=mate))

    last = {}

    def to_mate(n, j):
        u = n * block_rows + j
        last[u] = [fourth[u][-1]]
        for step in range(1, ways):
            fourth[u][step - 1].wait_recv()
            there = rows(n, j, lax.rem(y + ways - step, ways) * CORES + c)
            last[u].append(send(there, there, s5.at[u, step], r5.at[u, step], replica=mate))

    def multiply(m):
        k, j = m // block_rows, m % block_rows
        for n in range(k * subs, (k + 1) * subs):
            for copy in last.pop(n * block_rows + j):
                copy.wait_recv()
        left, right, lroot, rroot, update, block = held
        fetch = pltpu.make_async_copy(out.at[k, pl.ds(j * per_block, per_block)], block.at[m], block_sem.at[m])
        fetch.start()
        if m == 0:
            for load in loads[1:]:
                load.wait()
        fetch.wait()
        whole = block[m].reshape(width, width)
        columns_mine = block[m, :, :, :, lanes_of(share, r)].reshape(width, -1)
        strip_rows = ways * CORES * piece
        if share % strip_rows == 0:
            held_rows = block[m, pl.ds(r * (share // strip_rows), share // strip_rows)]
        else:
            first_piece = lax.div(lax.rem(r * share, strip_rows), piece)
            held_rows = block[m, lax.div(r * share, strip_rows), pl.ds(first_piece, share // piece)]
        value = products(share, r, whole, held_rows.reshape(share, width), columns_mine,
                         left.at[m], right.at[m], lroot.at[m], rroot.at[m])
        left[m], right[m], update[m] = value
        for i, source in enumerate((left, right, update)):
            stores.append(pltpu.make_async_copy(source.at[m], done[i].at[m], early_out.at[m, i]))
            stores[-1].start()

    stores = []
    for n in range(count):
        to_owners(n)
        if n + 2 < count:
            to_far(n + 2)
    for n in range(count):
        if n == min(1, count - 1):
            for late in range(max(count - 2, 0), count):
                to_near(late)
        k = n // subs
        for j in range(block_rows):
            if j and n % subs == subs - 1:
                multiply(k * block_rows + j - 1)
            to_mate(n, j)
        if n % subs == subs - 1 and (k + 1) * block_rows <= early:
            multiply((k + 1) * block_rows - 1)
    for copies in last.values():
        for copy in copies:
            copy.wait_recv()
    for copy in pending:
        copy.wait_send()
    loads[0].wait()
    for store in stores:
        store.wait()


def precondition(early, share, *refs):
    refs = list(refs)
    blocks, left, right, lroot, rroot = (refs.pop(0) for _ in range(5))
    ready = [refs.pop(0) for _ in range(3)] if early else []
    outs = [refs.pop(0) for _ in range(3)]
    block, mine, answer = refs.pop(0), [refs.pop(0) for _ in range(4)], refs.pop(0)
    in_sem, ready_sem, out_sem = refs
    r = lax.axis_index("replica")
    sources = [blocks.at[early], left.at[early], right.at[early], lroot, rroot.at[early]]
    fetches = [pltpu.make_async_copy(source, target, in_sem.at[i])
               for i, (source, target) in enumerate(zip(sources, [block] + mine))]
    for fetch in fetches:
        fetch.start()
    stores = []
    for i, source in enumerate(ready):
        stores.append(pltpu.make_async_copy(source, outs[i].at[pl.ds(0, early)], ready_sem.at[i]))
        stores[-1].start()
    for fetch in fetches:
        fetch.wait()
    rows = block[pl.ds(pl.multiple_of(r * share, 16), share), :]
    values = products(share, r, block[...], rows, block[:, lanes_of(share, r)], *mine)
    for i, target in enumerate((mine[0], mine[1], answer)):
        target[...] = values[i]
        stores.append(pltpu.make_async_copy(target, outs[i].at[early], out_sem.at[i]))
        stores[-1].start()
    for store in stores:
        store.wait()


def shards(gradients, left_factor, right_factor, left_root, right_root, owner_table):
    owners = lax.axis_size("fsdp")
    replicas = lax.axis_size("replica")
    ways = replicas // CORES
    strip_rows, total_cols = gradients.shape[1:]
    width = left_factor.shape[-1]
    depth, block_rows, share = left_factor.shape[1:4]
    columns = total_cols // width
    per_block = width // strip_rows
    piece = strip_rows // replicas
    sub = SUB if piece % SUB == 0 else piece
    chunks = depth * (piece // sub)
    hops = max(ways - 1, 1)
    total = depth * block_rows
    early = total - 1
    geo = (depth, owners, ways, piece, sub, width, per_block, columns, share, early)
    bf16 = jnp.bfloat16
    dma = pltpu.SemaphoreType.DMA
    vmem = [pltpu.VMEM(shape, kind) for shape, kind in (
        ((ways * piece, total_cols), bf16),
        ((hops, piece, total_cols), bf16),
        ((piece, total_cols), bf16),
        ((hops, columns, piece, width), bf16),
        ((columns, piece, width), jnp.float32),
        ((chunks, hops, owners, sub, width), bf16),
        ((chunks, hops, owners, sub, width), bf16),
        ((chunks, owners, sub, width), bf16),
    )]
    f32 = jnp.float32

    def parts(count):
        return [(count, share, width)] * 3 + [(count, width, width)]

    held = []
    if early:
        shapes = parts(early)
        held = [pltpu.VMEM(shape, kind) for shape, kind in zip(shapes, (f32, f32, bf16, bf16))]
        held += [pltpu.VMEM(shapes[0], bf16), pltpu.VMEM((early, per_block, replicas, piece, width), bf16)]
    planned = sum(math.prod(ref.shape) * jnp.dtype(ref.dtype).itemsize for ref in vmem + held) + 6 * 1024 * 1024
    given = [x.reshape(shape) for x, shape in
             zip((left_factor, right_factor, left_root, right_root), parts(total))]
    result = parts(total)[0]
    anywhere = pl.BlockSpec(memory_space=pl.ANY)
    first = [jax.ShapeDtypeStruct((depth, owners, replicas, piece, width), bf16),
             jax.ShapeDtypeStruct(result[1:], bf16)]
    if early:
        first += [jax.ShapeDtypeStruct((early,) + result[1:], kind) for kind in (f32, f32, bf16)]
    blocks, lroot, *ready = pl.pallas_call(
        functools.partial(exchange, geo),
        out_shape=tuple(first),
        in_specs=[pl.BlockSpec(memory_space=pltpu.HBM)] * 6,
        out_specs=(anywhere,) * len(first),
        scratch_shapes=held + [
            dma((5,)), dma((total, 3)), dma((total,)),
            pltpu.SMEM(owner_table.shape, jnp.int32),
            *vmem[:5],
            pltpu.SMEM((depth, owners), jnp.int32),
            pltpu.SMEM((depth, owners), jnp.int32),
            *vmem[5:],
            pltpu.SemaphoreType.REGULAR((4,)),
            dma, dma((ways,)),
            dma((ways, piece // sub)), dma((ways, piece // sub)),
            dma((chunks, ways)), dma((chunks, ways)),
            dma((chunks, owners)), dma((chunks, owners)),
            dma((chunks * block_rows, ways)), dma((chunks * block_rows, ways)),
            dma((chunks * block_rows, ways)), dma((chunks * block_rows, ways)),
            dma((chunks,)),
        ],
        compiler_params=pltpu.CompilerParams(collective_id=0, has_side_effects=True, vmem_limit_bytes=planned),
    )(*(pltpu.with_memory_space_constraint(x, pltpu.HBM) for x in [owner_table, gradients] + given))
    blocks = blocks.reshape(total, width, width)

    shapes = parts(1)
    outs = (jax.ShapeDtypeStruct(result, f32), jax.ShapeDtypeStruct(result, f32), jax.ShapeDtypeStruct(result, bf16))
    results = pl.pallas_call(
        functools.partial(precondition, early, share),
        out_shape=outs,
        in_specs=[anywhere] * (5 + len(ready)),
        out_specs=(anywhere,) * 3,
        scratch_shapes=[
            pltpu.VMEM((width, width), bf16),
            pltpu.VMEM(shapes[0][1:], f32),
            pltpu.VMEM(shapes[0][1:], f32),
            pltpu.VMEM(shapes[0][1:], bf16),
            pltpu.VMEM(shapes[3][1:], bf16),
            pltpu.VMEM(shapes[0][1:], bf16),
            dma((5,)), dma((3,)), dma((3,)),
        ],
        compiler_params=pltpu.CompilerParams(vmem_limit_bytes=20 * 1024 * 1024),
    )(blocks, given[0], given[1], lroot, given[3], *ready)
    return tuple(x.reshape(left_factor.shape) for x in results)


def solution(mesh):
    placed = (
        P("replica", "fsdp", None),
        P("fsdp", None, None, "replica", None),
        P("fsdp", None, None, "replica", None),
        P("fsdp", None, None, "replica", None),
        P("fsdp", None, None, None, None),
        P(),
    )
    factors = P("fsdp", None, None, "replica", None)
    return jax.shard_map(
        shards,
        mesh=mesh,
        in_specs=placed,
        out_specs=(factors, factors, factors),
        check_vma=False,
    )
```

```python
import functools
import math

import jax
import jax.numpy as jnp
from jax import lax
from jax.experimental import pallas as pl
from jax.experimental.pallas import tpu as pltpu
from jax.sharding import PartitionSpec as P

decay_rate = 0.9
MESH = pl.DeviceIdType.MESH
CORES = 2
SUB = 16


def lanes_of(share, r):
    lanes = max(share, 128)
    return pl.ds(pl.multiple_of(lax.div(r, lanes // share) * lanes, 128), lanes)


def products(share, r, whole, rows, columns, left, right, lroot, rroot):
    scale = (1.0 - decay_rate) / whole.shape[0]
    shares = columns.shape[1] // share
    f32 = jnp.float32
    stat_left = lax.dot_general(rows, whole, (((1,), (1,)), ((), ())), preferred_element_type=f32)
    left_new = decay_rate * left[...] + scale * stat_left
    stat_right = lax.dot_general(columns, whole, (((0,), (0,)), ((), ())), preferred_element_type=f32)
    mine = stat_right[:share]
    for i in range(1, shares):
        mine = jnp.where(lax.rem(r, shares) == i, stat_right[i * share:(i + 1) * share], mine)
    right_new = decay_rate * right[...] + scale * mine
    half = jnp.dot(lroot[...], whole, preferred_element_type=f32).astype(jnp.bfloat16)
    update = jnp.dot(half, rroot[...], preferred_element_type=f32).astype(jnp.bfloat16)
    return left_new, right_new, update


def exchange(geo, table, grad, *refs):
    refs = list(refs)
    given = [refs.pop(0) for _ in range(4)]
    out, kept = refs.pop(0), refs.pop(0)
    done = [refs.pop(0) for _ in range(3)] if geo[-1] else []
    held = [refs.pop(0) for _ in range(6)] if geo[-1] else []
    early_in, early_out, block_sem = (refs.pop(0) for _ in range(3))
    _exchange(geo, table, grad, given, out, kept, done, held, early_in, early_out, block_sem, *refs)


def _exchange(geo, table, grad, given, out, kept, done, held, early_in, early_out, block_sem,
              owner_of, strip, other, same, pair_far, pair_same, cols, live, near_out, near_in, ready,
              here, table_sem, load_sem, s1, r1, s2, r2, s3, r3, s4, r4, s5, r5, own_sem):
    depth, owners, ways, piece, sub, width, per_block, columns, share, early = geo
    subs = piece // sub
    chunks = [(k, i) for k in range(depth) for i in range(subs)]
    f = lax.axis_index("fsdp")
    r = lax.axis_index("replica")
    c, y = lax.rem(r, CORES), lax.div(r, CORES)
    mate = y * CORES + (1 - c)
    half = ways * piece

    def far_y(step):
        return lax.rem(y + step, ways)

    def far_f(step):
        if owners & (owners - 1):
            return lax.rem(f + step, owners)
        other_f, bit = f, 1
        while bit <= step:
            if step & bit:
                other_f = other_f + (1 - 2 * lax.rem(lax.div(f, bit), 2)) * bit
            bit *= 2
        return other_f

    barrier = pltpu.get_barrier_semaphore()
    met_mate, met_y, met_y_mates, met_owners = (here.at[i] for i in range(4))

    def tell(sem, **to):
        pl.semaphore_signal(sem, inc=1, device_id=to, device_id_type=MESH)

    @pl.when(c == 1)
    def side_enters():
        tell(barrier, replica=mate)

    @pl.when(c == 0)
    def lead_enters():
        for step in range(1, ways):
            tell(barrier, replica=far_y(step) * CORES)
        pl.semaphore_wait(barrier, ways)
        tell(met_mate, replica=mate)
        for step in range(1, ways):
            tell(met_y, replica=far_y(step) * CORES)

    @pl.when(c == 1)
    def side_goes_on():
        pl.semaphore_wait(met_mate, 1)
        for step in range(1, owners):
            tell(barrier, fsdp=far_f(step))

    names = pltpu.make_async_copy(table, owner_of, table_sem)
    names.start()

    pending = []

    def copy_to(src, dst, s, t, **to):
        return pltpu.make_async_remote_copy(
            src_ref=src, dst_ref=dst, send_sem=s, recv_sem=t, device_id=to, device_id_type=MESH
        )

    def send(src, dst, s, t, **to):
        copy = copy_to(src, dst, s, t, **to)
        copy.start()
        pending.append(copy)
        return copy

    pairs = {}

    def to_pair(step, i):
        into = other.at[step - 1, pl.ds(i * sub, sub)] if step else same.at[pl.ds(i * sub, sub)]
        start = pl.multiple_of((1 - c) * half + far_y(step) * piece + i * sub, 16)
        pairs[step, i] = send(grad.at[0, pl.ds(start, sub)], into, s1.at[step, i], r1.at[step, i], replica=mate)

    def near_rows(step):
        return pl.ds(pl.multiple_of(far_y(step) * piece, 16), piece)

    mine = {}
    for step in list(range(1, ways)) + [0]:
        for i in range(subs if step else 0):
            to_pair(step, i)
        start = pl.multiple_of(c * half + far_y(step) * piece, 16)
        mine[step] = pltpu.make_async_copy(grad.at[0, pl.ds(start, piece)], strip.at[near_rows(step)], load_sem.at[step])
        mine[step].start()
    @pl.when(c == 0)
    def lead_knows_y():
        if ways > 1:
            pl.semaphore_wait(met_y, ways - 1)
        tell(met_y_mates, replica=mate)

    names.wait()
    row = lax.div(f, per_block)

    names_here = [owner_of[row, col] for col in range(columns)]

    def place(d, carry):
        code = jnp.int32(0)
        for col in reversed(range(columns)):
            code = jnp.where(names_here[col] == d, code * (columns + 1) + (col + 1), code)
        for k in range(depth):
            digit = lax.rem(code, columns + 1)
            code = lax.div(code, columns + 1)
            cols[k, d] = jnp.maximum(digit - 1, 0)
            live[k, d] = jnp.minimum(digit, 1)
        return carry

    lax.fori_loop(0, owners, place, 0)

    def pair(step, i):
        pairs[step, i].wait_recv()
        low = pl.multiple_of(far_y(step) * piece + i * sub, 16)
        here = pl.ds(i * sub, sub)

        def add(col, carry):
            lanes = pl.ds(pl.multiple_of(col * width, 128), width)
            theirs = other[step - 1, here, lanes] if step else same[here, lanes]
            total = strip[pl.ds(low, sub), lanes].astype(jnp.float32) + theirs.astype(jnp.float32)
            if step:
                pair_far[step - 1, col, here, :] = total.astype(jnp.bfloat16)
            else:
                pair_same[col, here, :] = total
            return carry

        lax.fori_loop(0, columns, add, 0)

    second = {}

    def to_far(n):
        second[n] = []
        k, i = chunks[n]
        for step in range(1, ways):
            if k == 0:
                if i == 0:
                    mine[step].wait()
                pair(step, i)

            def pick(d, carry):
                near_out[n, step - 1, d] = pair_far[step - 1, cols[k, d], i * sub:(i + 1) * sub, :]
                return carry

            lax.fori_loop(0, owners, pick, 0)
            second[n].append(send(near_out.at[n, step - 1], near_in.at[n, step - 1], s2.at[n, step], r2.at[n, step],
                                  replica=far_y(step) * CORES + c))

    @pl.when(c == 1)
    def side_knows_y():
        pl.semaphore_wait(met_y_mates, 1)

    to_far(0)
    for i in range(subs):
        to_pair(0, i)
    if len(chunks) > 1:
        to_far(1)
    loads = [pltpu.make_async_copy(given[2].at[early], kept, early_in.at[0])]
    for i in range(4 if early else 0):
        loads.append(pltpu.make_async_copy(given[i].at[pl.ds(0, early)], held[i], early_in.at[i + 1]))
    for load in loads:
        load.start()
    mine[0].wait()
    for i in range(subs):
        pair(0, i)

    @pl.when(c == 1)
    def side_knows_owners():
        pl.semaphore_wait(barrier, owners - 1)
        tell(met_owners, replica=mate)

    @pl.when(c == 0)
    def lead_knows_owners():
        pl.semaphore_wait(met_owners, 1)

    block_rows = owners // per_block

    def rows(n, j, source):
        k, i = chunks[n]
        spot = lax.rem(source, CORES) * ways + lax.div(source, CORES)
        return out.at[k, pl.ds(j * per_block, per_block), spot, pl.ds(i * sub, sub)]

    def row_of(n, source):
        k, i = chunks[n]
        return out.at[k, source, c * ways + y, pl.ds(i * sub, sub)]

    def arrived(n, source):
        @pl.when(f != source)
        def wait():
            copy_to(ready.at[n, 0], row_of(n, source), s3.at[n, 0], r3.at[n, source], fsdp=far_f(1)).wait_recv()

    third = {}

    def to_owners(n):
        for copy in second[n]:
            copy.wait_recv()
        for step in reversed(range(owners)):
            d = far_f(step)
            k, i = chunks[n]
            total = pair_same[cols[k, d], i * sub:(i + 1) * sub, :]
            for other_y in range(1, ways):
                total = total + near_in[n, other_y - 1, d].astype(jnp.float32)
            total = total * live[chunks[n][0], d].astype(jnp.float32)
            ready[n, step] = total.astype(jnp.bfloat16)
            if step == 0:
                third[n] = pltpu.make_async_copy(ready.at[n, 0], row_of(n, f), own_sem.at[n])
                third[n].start()
            else:
                send(ready.at[n, step], row_of(n, f), s3.at[n, step], r3.at[n, f], fsdp=d)

    fourth = {}

    def to_near(n):
        third[n].wait()
        for j in range(block_rows):
            for q in range(per_block):
                arrived(n, j * per_block + q)
            u = n * block_rows + j
            mine_now = rows(n, j, r)
            fourth[u] = []
            for step in range(1, ways):
                fourth[u].append(send(mine_now, mine_now, s4.at[u, step], r4.at[u, step], replica=far_y(step) * CORES + c))
            fourth[u].append(send(mine_now, mine_now, s5.at[u, 0], r5.at[u, 0], replica=mate))

    last = {}

    def to_mate(n, j):
        u = n * block_rows + j
        last[u] = [fourth[u][-1]]
        for step in range(1, ways):
            fourth[u][step - 1].wait_recv()
            there = rows(n, j, lax.rem(y + ways - step, ways) * CORES + c)
            last[u].append(send(there, there, s5.at[u, step], r5.at[u, step], replica=mate))

    def multiply(m):
        k, j = m // block_rows, m % block_rows
        for n in range(k * subs, (k + 1) * subs):
            for copy in last.pop(n * block_rows + j):
                copy.wait_recv()
        left, right, lroot, rroot, update, block = held
        fetch = pltpu.make_async_copy(out.at[k, pl.ds(j * per_block, per_block)], block.at[m], block_sem.at[m])
        fetch.start()
        if m == 0:
            for load in loads[1:]:
                load.wait()
        fetch.wait()
        whole = block[m].reshape(width, width)
        columns_mine = block[m, :, :, :, lanes_of(share, r)].reshape(width, -1)
        strip_rows = ways * CORES * piece
        if share % strip_rows == 0:
            held_rows = block[m, pl.ds(r * (share // strip_rows), share // strip_rows)]
        else:
            first_piece = lax.div(lax.rem(r * share, strip_rows), piece)
            held_rows = block[m, lax.div(r * share, strip_rows), pl.ds(first_piece, share // piece)]
        value = products(share, r, whole, held_rows.reshape(share, width), columns_mine,
                         left.at[m], right.at[m], lroot.at[m], rroot.at[m])
        left[m], right[m], update[m] = value
        for i, source in enumerate((left, right, update)):
            stores.append(pltpu.make_async_copy(source.at[m], done[i].at[m], early_out.at[m, i]))
            stores[-1].start()

    stores = []
    count = len(chunks)
    for n in range(count):
        if n >= 2:
            to_near(n - 2)
        to_owners(n)
        if n + 2 < count:
            to_far(n + 2)
    for n in range(count):
        if n == min(1, count - 1):
            for late in range(max(count - 2, 0), count):
                to_near(late)
        k = n // subs
        for j in range(block_rows):
            to_mate(n, j)
            if j and n % subs == subs - 1:
                multiply(k * block_rows + j - 1)
        if n % subs == subs - 1 and (k + 1) * block_rows <= early:
            multiply((k + 1) * block_rows - 1)
    for copies in last.values():
        for copy in copies:
            copy.wait_recv()
    for copy in pending:
        copy.wait_send()
    loads[0].wait()
    for store in stores:
        store.wait()


def precondition(early, share, *refs):
    refs = list(refs)
    blocks, left, right, lroot, rroot = (refs.pop(0) for _ in range(5))
    ready = [refs.pop(0) for _ in range(3)] if early else []
    outs = [refs.pop(0) for _ in range(3)]
    block, mine, answer = refs.pop(0), [refs.pop(0) for _ in range(4)], refs.pop(0)
    in_sem, ready_sem, out_sem = refs
    r = lax.axis_index("replica")
    sources = [blocks.at[early], left.at[early], right.at[early], lroot, rroot.at[early]]
    fetches = [pltpu.make_async_copy(source, target, in_sem.at[i])
               for i, (source, target) in enumerate(zip(sources, [block] + mine))]
    for fetch in fetches:
        fetch.start()
    stores = []
    for i, source in enumerate(ready):
        stores.append(pltpu.make_async_copy(source, outs[i].at[pl.ds(0, early)], ready_sem.at[i]))
        stores[-1].start()
    for fetch in fetches:
        fetch.wait()
    rows = block[pl.ds(pl.multiple_of(r * share, 16), share), :]
    values = products(share, r, block[...], rows, block[:, lanes_of(share, r)], *mine)
    for i, target in enumerate((mine[0], mine[1], answer)):
        target[...] = values[i]
        stores.append(pltpu.make_async_copy(target, outs[i].at[early], out_sem.at[i]))
        stores[-1].start()
    for store in stores:
        store.wait()


def shards(gradients, left_factor, right_factor, left_root, right_root, owner_table):
    owners = lax.axis_size("fsdp")
    replicas = lax.axis_size("replica")
    ways = replicas // CORES
    strip_rows, total_cols = gradients.shape[1:]
    width = left_factor.shape[-1]
    depth, block_rows, share = left_factor.shape[1:4]
    columns = total_cols // width
    per_block = width // strip_rows
    piece = strip_rows // replicas
    sub = SUB if piece % SUB == 0 else piece
    chunks = depth * (piece // sub)
    hops = max(ways - 1, 1)
    total = depth * block_rows
    early = total - 1
    geo = (depth, owners, ways, piece, sub, width, per_block, columns, share, early)
    bf16 = jnp.bfloat16
    dma = pltpu.SemaphoreType.DMA
    vmem = [pltpu.VMEM(shape, kind) for shape, kind in (
        ((ways * piece, total_cols), bf16),
        ((hops, piece, total_cols), bf16),
        ((piece, total_cols), bf16),
        ((hops, columns, piece, width), bf16),
        ((columns, piece, width), jnp.float32),
        ((chunks, hops, owners, sub, width), bf16),
        ((chunks, hops, owners, sub, width), bf16),
        ((chunks, owners, sub, width), bf16),
    )]
    f32 = jnp.float32

    def parts(count):
        return [(count, share, width)] * 3 + [(count, width, width)]

    held = []
    if early:
        shapes = parts(early)
        held = [pltpu.VMEM(shape, kind) for shape, kind in zip(shapes, (f32, f32, bf16, bf16))]
        held += [pltpu.VMEM(shapes[0], bf16), pltpu.VMEM((early, per_block, replicas, piece, width), bf16)]
    planned = sum(math.prod(ref.shape) * jnp.dtype(ref.dtype).itemsize for ref in vmem + held) + 6 * 1024 * 1024
    given = [x.reshape(shape) for x, shape in
             zip((left_factor, right_factor, left_root, right_root), parts(total))]
    result = parts(total)[0]
    anywhere = pl.BlockSpec(memory_space=pl.ANY)
    first = [jax.ShapeDtypeStruct((depth, owners, replicas, piece, width), bf16),
             jax.ShapeDtypeStruct(result[1:], bf16)]
    if early:
        first += [jax.ShapeDtypeStruct((early,) + result[1:], kind) for kind in (f32, f32, bf16)]
    blocks, lroot, *ready = pl.pallas_call(
        functools.partial(exchange, geo),
        out_shape=tuple(first),
        in_specs=[pl.BlockSpec(memory_space=pltpu.HBM)] * 6,
        out_specs=(anywhere,) * len(first),
        scratch_shapes=held + [
            dma((5,)), dma((total, 3)), dma((total,)),
            pltpu.SMEM(owner_table.shape, jnp.int32),
            *vmem[:5],
            pltpu.SMEM((depth, owners), jnp.int32),
            pltpu.SMEM((depth, owners), jnp.int32),
            *vmem[5:],
            pltpu.SemaphoreType.REGULAR((4,)),
            dma, dma((ways,)),
            dma((ways, piece // sub)), dma((ways, piece // sub)),
            dma((chunks, ways)), dma((chunks, ways)),
            dma((chunks, owners)), dma((chunks, owners)),
            dma((chunks * block_rows, ways)), dma((chunks * block_rows, ways)),
            dma((chunks * block_rows, ways)), dma((chunks * block_rows, ways)),
            dma((chunks,)),
        ],
        compiler_params=pltpu.CompilerParams(collective_id=0, has_side_effects=True, vmem_limit_bytes=planned),
    )(*(pltpu.with_memory_space_constraint(x, pltpu.HBM) for x in [owner_table, gradients] + given))
    blocks = blocks.reshape(total, width, width)

    shapes = parts(1)
    outs = (jax.ShapeDtypeStruct(result, f32), jax.ShapeDtypeStruct(result, f32), jax.ShapeDtypeStruct(result, bf16))
    results = pl.pallas_call(
        functools.partial(precondition, early, share),
        out_shape=outs,
        in_specs=[anywhere] * (5 + len(ready)),
        out_specs=(anywhere,) * 3,
        scratch_shapes=[
            pltpu.VMEM((width, width), bf16),
            pltpu.VMEM(shapes[0][1:], f32),
            pltpu.VMEM(shapes[0][1:], f32),
            pltpu.VMEM(shapes[0][1:], bf16),
            pltpu.VMEM(shapes[3][1:], bf16),
            pltpu.VMEM(shapes[0][1:], bf16),
            dma((5,)), dma((3,)), dma((3,)),
        ],
        compiler_params=pltpu.CompilerParams(vmem_limit_bytes=20 * 1024 * 1024),
    )(blocks, given[0], given[1], lroot, given[3], *ready)
    return tuple(x.reshape(left_factor.shape) for x in results)


def solution(mesh):
    placed = (
        P("replica", "fsdp", None),
        P("fsdp", None, None, "replica", None),
        P("fsdp", None, None, "replica", None),
        P("fsdp", None, None, "replica", None),
        P("fsdp", None, None, None, None),
        P(),
    )
    factors = P("fsdp", None, None, "replica", None)
    return jax.shard_map(
        shards,
        mesh=mesh,
        in_specs=placed,
        out_specs=(factors, factors, factors),
        check_vma=False,
    )
```
